512 devices in a mesh: dp: 4 (over z_hi), context: 128 (over z_lo, y, x, core).
Axes of the slice: x: 4, y: 4, z: 16 (z_hi: 4, z_lo: 4; z = z_hi * 4 + z_lo), core: 2. Of those that a mesh axis runs over, the one named last changes fastest.
Arguments:
- input_gate: bfloat16 [4, 16384, 256], P('dp', 'context'), may hold values from -6 to 6
- values: bfloat16 [4, 16384, 256], P('dp', 'context'), may hold values from -6 to 6
- output_gate: bfloat16 [4, 16384, 256], P('dp', 'context'), may hold values from -6 to 6
- grad_out: bfloat16 [4, 16384, 256], P('dp', 'context'), may hold values from -6 to 6
- filter_taps: bfloat16 [256, 16384], P('context'), may hold values from -0.046875 to 0.046875
- skip_gain: float32 [256], replicated, may hold values from -4 to 4
Outputs:
- grad_input_gate: bfloat16 [4, 16384, 256], P('dp', 'context')
- grad_values: bfloat16 [4, 16384, 256], P('dp', 'context')
- grad_output_gate: bfloat16 [4, 16384, 256], P('dp', 'context')
- filter_grad: float32 [256, 16384], P('context', 'dp')
- skip_grad: float32 [256], replicated
The draws below stay inside these ranges and needn't reach their ends.
All inputs are finite; a program needn't handle non-finite values.
Results may differ from the reference program's by a relative error of at most 0.014.
Values may be sent and summed in bfloat16 or wider, within the bound.
A program may use at most 64 MiB of HBM per device.

```python
import math
import jax
import jax.numpy as jnp
from jax import lax

C = 256
L = 16384
SEQS = 4
N_CONTEXT = 128


def block_levels(stream_key, extent, shards, smallest, largest):
    level = 1.0
    for axis_at, blocks in shards:
        draws = jax.random.uniform(jax.random.fold_in(jax.random.fold_in(stream_key, 6), axis_at), (blocks,), jnp.float32, smallest / len(shards), largest / len(shards))
        level = level * jnp.repeat(jnp.exp(draws), extent[axis_at] // blocks).reshape((-1,) + (1,) * (len(extent) - 1 - axis_at))
    return level


def noise(rng, extent, scale, bound, cuts=(), kind=jnp.bfloat16):
    entries = jax.random.normal(rng, extent, jnp.float32) * scale
    if len(cuts) > 0:
        entries = block_levels(rng, extent, cuts, -0.22, 0.18) * entries
    return jnp.clip(entries, min=-bound, max=bound).astype(kind)


def setup_inputs(seed: int = 0) -> dict:
    streams_of = jax.random.split(jax.random.key(seed), 7)
    input_gate = noise(streams_of[0], (SEQS, L, C), 1.0, 6.0, ((0, 4), (1, 128)))
    values = noise(streams_of[1], (SEQS, L, C), 1.0, 6.0, ((0, 4), (1, 128)))
    output_gate = noise(streams_of[2], (SEQS, L, C), 1.0, 6.0, ((0, 4), (1, 128)))
    grad_out = noise(streams_of[3], (SEQS, L, C), 1.0, 6.0, ((0, 4), (1, 128)))
    filter_taps = noise(streams_of[4], (C, L), L ** -0.5, 0.046875, ((0, 128),))
    skip_gain = noise(streams_of[5], (C,), 1.0, 4.0, (), jnp.float32)
    return {"input_gate": input_gate, "values": values, "output_gate": output_gate, "grad_out": grad_out, "filter_taps": filter_taps, "skip_gain": skip_gain}


def dft_tables(pieces, block_len):
    outer = 2 * pieces
    total = outer * block_len

    def phase(first, second, modulus):
        product = first[:, None] * second[None, :] % modulus
        return product.astype(jnp.float32) * (2.0 * math.pi / modulus)
    across = jnp.arange(pieces, dtype=jnp.int32)
    outer_index = jnp.arange(outer, dtype=jnp.int32)
    inner_index = jnp.arange(block_len, dtype=jnp.int32)
    first_angle = phase(outer_index, across, outer)
    entry = jnp.stack([jnp.cos(first_angle), -jnp.sin(first_angle)]).astype(jnp.bfloat16)
    twist_angle = phase(outer_index, inner_index, total)
    twist_cos = jnp.cos(twist_angle)
    twist_sin = jnp.sin(twist_angle)
    inner_angle = phase(inner_index, inner_index, block_len)
    cosine = jnp.cos(inner_angle)
    sine = jnp.sin(inner_angle)
    forward_inner = jnp.stack([jnp.stack([cosine, -sine], 1), jnp.stack([sine, cosine], 1)]).astype(jnp.bfloat16)
    inverse_inner = jnp.stack([jnp.stack([cosine, sine], 1), jnp.stack([-sine, cosine], 1)]).astype(jnp.bfloat16)
    last_angle = phase(across, outer_index, outer)
    leave = jnp.stack([jnp.cos(last_angle), -jnp.sin(last_angle)], 1).astype(jnp.bfloat16)
    return (entry, twist_cos, twist_sin, forward_inner, inverse_inner, leave, 1.0 / total)

def transform(signal, tables):
    entry, twist_cos, twist_sin, forward_inner = (tables[0], tables[1], tables[2], tables[3])
    pieces = entry.shape[2]
    block_len = twist_cos.shape[1]
    shaped = signal.reshape(signal.shape[0], pieces, block_len).astype(jnp.float32)
    section = jnp.einsum('pka,rab->prkb', entry.astype(jnp.float32), shaped, precision=lax.Precision.HIGHEST)
    real_part = section[0] * twist_cos + section[1] * twist_sin
    imag_part = section[1] * twist_cos - section[0] * twist_sin
    turned = jnp.stack([real_part, imag_part]).astype(jnp.bfloat16)
    return jnp.einsum('prkb,pbqm->qrkm', turned.astype(jnp.float32), forward_inner.astype(jnp.float32), precision=lax.Precision.HIGHEST)

def untransform(spectrum, tables):
    twist_cos, twist_sin, inverse_inner, leave, scale = (tables[1], tables[2], tables[4], tables[5], tables[6])
    section = jnp.einsum('prkm,pmqb->qrkb', spectrum.astype(jnp.float32), inverse_inner.astype(jnp.float32), precision=lax.Precision.HIGHEST)
    real_part = section[0] * twist_cos - section[1] * twist_sin
    imag_part = section[1] * twist_cos + section[0] * twist_sin
    turned = jnp.stack([real_part, imag_part]).astype(jnp.bfloat16)
    result = jnp.einsum('apk,prkb->rab', leave.astype(jnp.float32), turned.astype(jnp.float32), precision=lax.Precision.HIGHEST)
    return (result * scale).reshape(result.shape[0], -1)

def spectral_products(source, kernel, incoming):
    forward_conv = jnp.stack([source[0] * kernel[0] - source[1] * kernel[1], source[0] * kernel[1] + source[1] * kernel[0]]).astype(jnp.bfloat16)
    backward_conv = jnp.stack([kernel[0] * incoming[0] + kernel[1] * incoming[1], kernel[0] * incoming[1] - kernel[1] * incoming[0]]).astype(jnp.bfloat16)
    kernel_grad = jnp.stack([source[0] * incoming[0] + source[1] * incoming[1], source[0] * incoming[1] - source[1] * incoming[0]]).astype(jnp.bfloat16)
    return (forward_conv, backward_conv, kernel_grad)

def reference(input_gate, values, output_gate, grad_out, filter_taps, skip_gain):
    seqs, length, chans = input_gate.shape
    pieces = N_CONTEXT
    block_len = length // pieces
    tables = dft_tables(pieces, block_len)
    mixed = (input_gate.astype(jnp.float32) * values.astype(jnp.float32)).astype(jnp.bfloat16)
    grad_mix = (grad_out.astype(jnp.float32) * output_gate.astype(jnp.float32)).astype(jnp.bfloat16)
    width = 16
    count = chans // width
    mixed_cols = mixed.transpose(2, 0, 1).reshape(count, width * seqs, length)
    grad_cols = grad_mix.transpose(2, 0, 1).reshape(count, width * seqs, length)
    taps = filter_taps.reshape(count, width, length)

    def one_block(inputs):
        mixed_block, grad_block, tap_block = inputs
        source = transform(mixed_block, tables)
        incoming = transform(grad_block, tables)
        kernel = jnp.repeat(transform(tap_block, tables), seqs, axis=1)
        forward_conv, backward_conv, kernel_grad = spectral_products(source, kernel, incoming)
        conv_out = untransform(forward_conv, tables).astype(jnp.bfloat16)
        conv_back = untransform(backward_conv, tables).astype(jnp.bfloat16)
        filter_term = untransform(kernel_grad, tables).reshape(width, seqs, length)
        return (conv_out, conv_back, lax.optimization_barrier(jnp.sum(filter_term, axis=1)))
    conv_out, conv_back, filter_sum = lax.map(one_block, (mixed_cols, grad_cols, taps))
    conv_out = conv_out.reshape(chans, seqs, length).transpose(1, 2, 0)
    conv_back = conv_back.reshape(chans, seqs, length).transpose(1, 2, 0)
    scale = 1.0 / math.sqrt(seqs * length)
    gated = conv_out.astype(jnp.float32) + skip_gain * mixed.astype(jnp.float32)
    grad_output_gate = (grad_out.astype(jnp.float32) * gated).astype(jnp.bfloat16)
    grad_mixed = conv_back.astype(jnp.float32) + skip_gain * grad_mix.astype(jnp.float32)
    grad_input_gate = (grad_mixed * values.astype(jnp.float32)).astype(jnp.bfloat16)
    grad_values = (grad_mixed * input_gate.astype(jnp.float32)).astype(jnp.bfloat16)
    filter_grad = filter_sum.reshape(chans, length) * scale
    skip_grad = lax.optimization_barrier(jnp.sum(grad_mix.astype(jnp.float32) * mixed.astype(jnp.float32), axis=(0, 1))) * scale
    return (grad_input_gate, grad_values, grad_output_gate, filter_grad, skip_grad)
```

```python
import functools
import math

import jax
import jax.numpy as jnp
import numpy as np
from jax import lax
from jax.experimental import pallas as pl
from jax.experimental.pallas import tpu as pltpu
from jax.sharding import PartitionSpec as P

MESH = pl.DeviceIdType.MESH
F32 = jnp.float32
BF16 = jnp.bfloat16


def group_sizes(context):
    near = 1
    while 2 * near * near * 2 <= context:
        near *= 2
    return context // near, near


def dft_tables(pieces, block_len, rows, scale):
    outer = 2 * pieces
    total = outer * block_len

    def angle(first, second, modulus):
        return (first[:, None] * second[None, :] % modulus) * (2.0 * math.pi / modulus)

    across = np.arange(pieces)
    outer_index = np.arange(outer)
    inner_index = np.arange(block_len)
    first = angle(outer_index, across, outer)
    entry = np.concatenate([np.cos(first), -np.sin(first)], 0)
    twist = angle(outer_index, inner_index, total)
    twist_cos, twist_sin = np.cos(twist), np.sin(twist)
    inner = angle(inner_index, inner_index, block_len)
    cosine, sine = np.cos(inner), np.sin(inner)
    forward_inner = np.block([[cosine, -sine], [sine, cosine]])
    inverse_inner = np.block([[cosine, sine], [-sine, cosine]])
    last = angle(across, outer_index, outer)
    leave = np.concatenate([np.cos(last), -np.sin(last)], 1) * scale

    def low(table):
        return jnp.asarray(table.astype(np.float32), dtype=BF16)

    return (
        low(entry[:, rows]),
        low(entry),
        jnp.asarray(twist_cos.astype(np.float32)),
        jnp.asarray(twist_sin.astype(np.float32)),
        low(forward_inner),
        low(inverse_inner),
        low(leave[rows]),
        low(leave),
    )


def dot(a, b):
    return jnp.dot(a, b, preferred_element_type=F32)


def flip(x):
    n = x.shape[1]
    eye = (
        lax.broadcasted_iota(jnp.int32, (n, n), 0) == lax.broadcasted_iota(jnp.int32, (n, n), 1)
    ).astype(BF16)
    return lax.dot_general(
        eye, x, (((1,), (1,)), ((), ())), preferred_element_type=F32
    ).astype(BF16)


def regroup(x, outer, inner):
    n = outer * inner
    row = lax.broadcasted_iota(jnp.int32, (n, n), 0)
    col = lax.broadcasted_iota(jnp.int32, (n, n), 1)
    place = (col == (row % outer) * inner + row // outer).astype(BF16)
    return dot(place, x).astype(BF16)


def mixer_kernel(
    sizes,
    ig_hbm, va_hbm, og_hbm, go_hbm, taps_hbm, entry_hbm, entry_nat_hbm, cos_hbm, sin_hbm,
    fwd_hbm, inv_hbm, leave_hbm, leave_nat_hbm,
    conv_ref, back_ref, filter_ref, skip_ref,
    ig, va, og, go, taps, entry, entry_nat, cos, sin, fwd, inv, leave, leave_nat,
    send1, recv1, send2, recv2, send3, recv3, send4, recv4,
    fsend, frecv, sdp, sdp_recv, s3, s3_recv, s4, s4_recv, kern,
    load_sem, send_sem, recv_sem,
):
    n_dp, far, near, chans, block = sizes
    ctx = far * near
    outer = 2 * ctx
    d = lax.axis_index("dp")
    c = lax.axis_index("context")
    g = c // near
    h = c % near

    pairs = (
        (ig_hbm, ig), (va_hbm, va), (og_hbm, og), (go_hbm, go), (taps_hbm, taps),
        (entry_nat_hbm, entry_nat), (cos_hbm, cos), (sin_hbm, sin), (fwd_hbm, fwd),
        (entry_hbm, entry), (inv_hbm, inv), (leave_hbm, leave), (leave_nat_hbm, leave_nat),
    )
    loads = [pltpu.make_async_copy(src, dst, load_sem.at[i]) for i, (src, dst) in enumerate(pairs)]
    for load in loads:
        load.start()

    def far_peer(i):
        t = (g + i) % far
        return t, (d, t * near + h)

    def near_peer(i):
        t = (h + i) % near
        return t, (d, g * near + t)

    def dp_peer(i):
        t = (d + i) % n_dp
        return t, (t, c)

    barrier = pltpu.get_barrier_semaphore()

    def greet(peer):
        def step(i, carry):
            pl.semaphore_signal(barrier, inc=1, device_id=peer(i)[1], device_id_type=MESH)
            return carry

        return step

    lax.fori_loop(1, far, greet(far_peer), 0)
    lax.fori_loop(1, near, greet(near_peer), 0)
    lax.fori_loop(1, n_dp, greet(dp_peer), 0)

    def send_all(peer, count, src, dst, own, sem):
        def step(i, carry):
            t, target = peer(i)
            pltpu.make_async_remote_copy(
                src_ref=src(t),
                dst_ref=dst.at[own],
                send_sem=send_sem.at[sem],
                recv_sem=recv_sem.at[sem],
                device_id=target,
                device_id_type=MESH,
            ).start()
            return carry

        lax.fori_loop(1, count, step, 0)

    def wait_blocks(dst, count, sem):
        part = dst.at[pl.ds(0, count - 1)]
        pltpu.make_async_copy(part, part, sem).wait()

    for i in range(4):
        loads[i].wait()
    mixed = (ig[...].astype(F32) * va[...].astype(F32)).astype(BF16)
    gmix = (go[...].astype(F32) * og[...].astype(F32)).astype(BF16)
    cols = flip(jnp.concatenate([mixed, gmix], 0))
    send1[:, 0] = cols[:, :block].reshape(far, 2 * near, block)
    send1[:, 1] = cols[:, block:].reshape(far, 2 * near, block)
    recv1[g] = send1[g]

    pl.semaphore_wait(barrier, far + near + n_dp - 3)
    send_all(far_peer, far, lambda t: send1.at[t], recv1, g, 0)

    def forward(table, x):
        section = dot(table, x)
        out = []
        for i in range(x.shape[1] // block):
            re = section[:outer, i * block : (i + 1) * block]
            im = section[outer:, i * block : (i + 1) * block]
            turned = jnp.concatenate(
                [
                    (re * cos[...] + im * sin[...]).astype(BF16),
                    (im * cos[...] - re * sin[...]).astype(BF16),
                ],
                1,
            )
            out.append(dot(turned, fwd[...]))
        return out

    def inverse(table, spectra):
        real, imag = [], []
        for spectrum in spectra:
            back = dot(spectrum, inv[...])
            re, im = back[:, :block], back[:, block:]
            real.append((re * cos[...] - im * sin[...]).astype(BF16))
            imag.append((im * cos[...] + re * sin[...]).astype(BF16))
        turned = jnp.concatenate([jnp.concatenate(real, 1), jnp.concatenate(imag, 1)], 0)
        return dot(table, turned)

    for i in range(4, 9):
        loads[i].wait()
    for j, spectrum in enumerate(
        forward(entry_nat[...], jnp.concatenate([taps[0], taps[1]], 1))
    ):
        kern[j] = spectrum

    wait_blocks(recv1, far, recv_sem.at[0])
    rows = jnp.concatenate(
        [recv1[:, 0].reshape(chans, block), recv1[:, 1].reshape(chans, block)], 1
    )
    rows = regroup(rows, far, 2 * near)
    send2[:, 0] = rows[:, :block].reshape(near, 2, far, block)
    send2[:, 1] = rows[:, block:].reshape(near, 2, far, block)
    recv2[h] = send2[h]
    send_all(near_peer, near, lambda t: send2.at[t], recv2, h, 1)

    for i in range(9, 13):
        loads[i].wait()
    wait_blocks(recv2, near, recv_sem.at[1])

    halves = []
    for j in range(2):
        a = recv2[:, 0, j].reshape(ctx, block)
        b = recv2[:, 1, j].reshape(ctx, block)
        halves.append((a, b))
        sdp[pl.ds(j, 1)] = jnp.sum(a.astype(F32) * b.astype(F32), axis=0, keepdims=True)
    sdp_recv[d] = sdp[...]
    send_all(dp_peer, n_dp, lambda t: sdp, sdp_recv, d, 2)

    filter_specs = []
    for j in range(2):
        u, v = forward(entry[...], jnp.concatenate(halves[j], 1))
        k = kern[j]
        ur, ui = u[:, :block], u[:, block:]
        vr, vi = v[:, :block], v[:, block:]
        kr, ki = k[:, :block], k[:, block:]
        conv = jnp.concatenate([ur * kr - ui * ki, ur * ki + ui * kr], 1).astype(BF16)
        back = jnp.concatenate([kr * vr + ki * vi, kr * vi - ki * vr], 1).astype(BF16)
        filter_specs.append(
            jnp.concatenate([ur * vr + ui * vi, ur * vi - ui * vr], 1).astype(BF16)
        )
        both = inverse(leave[...], [conv, back]).astype(BF16)
        send3[:, 0, j] = both[:, :block].reshape(near, far, block)
        send3[:, 1, j] = both[:, block:].reshape(near, far, block)
    recv3[h] = send3[h]
    send_all(near_peer, near, lambda t: send3.at[t], recv3, h, 3)

    wait_blocks(sdp_recv, n_dp, recv_sem.at[2])
    total = sdp_recv[0]
    for i in range(1, n_dp):
        total = total + sdp_recv[i]
    total = jnp.sum(total, axis=1, keepdims=True) * (1.0 / math.sqrt(n_dp * ctx * block))
    channel = lax.broadcasted_iota(jnp.int32, (2, 128), 0) * 128 + lax.broadcasted_iota(
        jnp.int32, (2, 128), 1
    )
    zero = jnp.zeros((2, 128), F32)
    s3[...] = jnp.where(channel == 2 * c, total[0:1], zero) + jnp.where(
        channel == 2 * c + 1, total[1:2], zero
    )
    s3_recv[h] = s3[...]
    send_all(near_peer, near, lambda t: s3, s3_recv, h, 4)

    term = inverse(leave_nat[...], filter_specs).astype(BF16)
    fsend[:, 0] = term[:, :block].reshape(n_dp, ctx // n_dp, block)
    fsend[:, 1] = term[:, block:].reshape(n_dp, ctx // n_dp, block)
    frecv[d] = fsend[d]
    send_all(dp_peer, n_dp, lambda t: fsend.at[t], frecv, d, 5)

    wait_blocks(recv3, near, recv_sem.at[3])
    rows = jnp.concatenate(
        [recv3[:, 0].reshape(chans, block), recv3[:, 1].reshape(chans, block)], 1
    )
    rows = regroup(rows, 2 * near, far)
    send4[:, 0] = rows[:, :block].reshape(far, 2 * near, block)
    send4[:, 1] = rows[:, block:].reshape(far, 2 * near, block)
    recv4[g] = send4[g]
    send_all(far_peer, far, lambda t: send4.at[t], recv4, g, 6)

    wait_blocks(s3_recv, near, recv_sem.at[4])
    total = s3_recv[0]
    for i in range(1, near):
        total = total + s3_recv[i]
    s4[...] = total
    s4_recv[g] = total
    send_all(far_peer, far, lambda t: s4, s4_recv, g, 7)

    wait_blocks(frecv, n_dp, recv_sem.at[5])
    grad = frecv[0].astype(F32)
    for i in range(1, n_dp):
        grad = grad + frecv[i].astype(F32)
    filter_ref[...] = grad * (1.0 / math.sqrt(n_dp * ctx * block))

    wait_blocks(recv4, far, recv_sem.at[6])
    tokens = flip(
        jnp.concatenate(
            [recv4[:, 0].reshape(chans, block), recv4[:, 1].reshape(chans, block)], 1
        )
    )
    conv_ref[...] = tokens[:block]
    back_ref[...] = tokens[block:]

    wait_blocks(s4_recv, far, recv_sem.at[7])
    total = s4_recv[0]
    for i in range(1, far):
        total = total + s4_recv[i]
    skip_ref[...] = total

    wait_blocks(recv1, far, send_sem.at[0])
    wait_blocks(recv2, near, send_sem.at[1])
    wait_blocks(sdp_recv, n_dp, send_sem.at[2])
    wait_blocks(recv3, near, send_sem.at[3])
    wait_blocks(s3_recv, near, send_sem.at[4])
    wait_blocks(frecv, n_dp, send_sem.at[5])
    wait_blocks(recv4, far, send_sem.at[6])
    wait_blocks(s4_recv, far, send_sem.at[7])


def per_device(input_gate, values, output_gate, grad_out, filter_taps, skip_gain):
    n_dp = lax.axis_size("dp")
    ctx = lax.axis_size("context")
    far, near = group_sizes(ctx)
    block, chans = input_gate.shape[1:]
    rows = np.arange(ctx).reshape(far, near).T.reshape(-1)
    tables = dft_tables(ctx, block, rows, 1.0 / (2 * ctx * block))
    gates = (input_gate[0], values[0], output_gate[0], grad_out[0])
    operands = gates + (filter_taps.reshape(-1, ctx, block),) + tables
    share = ctx // n_dp
    outs = (
        jax.ShapeDtypeStruct((block, chans), BF16),
        jax.ShapeDtypeStruct((block, chans), BF16),
        jax.ShapeDtypeStruct((2, share, block), F32),
        jax.ShapeDtypeStruct((2, 128), F32),
    )
    vmem = pltpu.VMEM
    conv_out, conv_back, filter_grad, skip_grad = pl.pallas_call(
        functools.partial(mixer_kernel, (n_dp, far, near, chans, block)),
        out_shape=outs,
        in_specs=[pl.BlockSpec(memory_space=pl.ANY)] * len(operands),
        out_specs=tuple(pl.BlockSpec(memory_space=pltpu.VMEM) for _ in outs),
        scratch_shapes=[vmem(x.shape, x.dtype) for x in operands]
        + [vmem((far, 2, 2 * near, block), BF16)] * 2
        + [vmem((near, 2, 2, far, block), BF16)] * 4
        + [vmem((far, 2, 2 * near, block), BF16)] * 2
        + [vmem((n_dp, 2, share, block), BF16)] * 2
        + [vmem((2, block), F32), vmem((n_dp, 2, block), F32)]
        + [vmem((2, 128), F32), vmem((near, 2, 128), F32)]
        + [vmem((2, 128), F32), vmem((far, 2, 128), F32)]
        + [vmem((2, 2 * ctx, 2 * block), F32)]
        + [
            pltpu.SemaphoreType.DMA((len(operands),)),
            pltpu.SemaphoreType.DMA((8,)),
            pltpu.SemaphoreType.DMA((8,)),
        ],
        compiler_params=pltpu.CompilerParams(
            collective_id=0, has_side_effects=True, vmem_limit_bytes=48 * 1024 * 1024
        ),
        name="mixer",
    )(*operands)

    gate_in, value, gate_out, cotangent = (x.astype(F32) for x in gates)
    mixed = (gate_in * value).astype(BF16).astype(F32)
    grad_mix = (cotangent * gate_out).astype(BF16).astype(F32)
    grad_output = (cotangent * (conv_out.astype(F32) + skip_gain * mixed)).astype(BF16)
    grad_mixed = conv_back.astype(F32) + skip_gain * grad_mix
    grad_input = (grad_mixed * value).astype(BF16)
    grad_value = (grad_mixed * gate_in).astype(BF16)
    return (
        grad_input[None],
        grad_value[None],
        grad_output[None],
        filter_grad.reshape(2, share * block),
        skip_grad.reshape(-1)[:chans],
    )


def solution(mesh):
    return jax.shard_map(
        per_device,
        mesh=mesh,
        in_specs=(
            P("dp", "context", None),
            P("dp", "context", None),
            P("dp", "context", None),
            P("dp", "context", None),
            P("context", None),
            P(),
        ),
        out_specs=(
            P("dp", "context", None),
            P("dp", "context", None),
            P("dp", "context", None),
            P("context", "dp"),
            P(),
        ),
        check_vma=False,
    )
```

```python
import functools
import math

import jax
import jax.numpy as jnp
import numpy as np
from jax import lax
from jax.experimental import pallas as pl
from jax.experimental.pallas import tpu as pltpu
from jax.sharding import PartitionSpec as P

MESH = pl.DeviceIdType.MESH
F32 = jnp.float32
BF16 = jnp.bfloat16
UNROLL = False


def group_sizes(context):
    near = 1
    while 2 * near * near * 2 <= context:
        near *= 2
    return context // near, near


def dft_tables(pieces, block_len, rows, scale):
    outer = 2 * pieces
    total = outer * block_len

    def angle(first, second, modulus):
        return (first[:, None] * second[None, :] % modulus) * (2.0 * math.pi / modulus)

    across = np.arange(pieces)
    outer_index = np.arange(outer)
    inner_index = np.arange(block_len)
    first = angle(outer_index, across, outer)
    entry = np.concatenate([np.cos(first), -np.sin(first)], 0)
    twist = angle(outer_index, inner_index, total)
    twist_cos, twist_sin = np.cos(twist), np.sin(twist)
    inner = angle(inner_index, inner_index, block_len)
    cosine, sine = np.cos(inner), np.sin(inner)
    forward_inner = np.block([[cosine, -sine], [sine, cosine]])
    inverse_inner = np.block([[cosine, sine], [-sine, cosine]])
    last = angle(across, outer_index, outer)
    leave = np.concatenate([np.cos(last), -np.sin(last)], 1) * scale

    def low(table):
        return table.astype(BF16).astype(np.float32)

    return (
        low(entry),
        twist_cos.astype(np.float32),
        twist_sin.astype(np.float32),
        low(forward_inner),
        low(entry[:, rows]),
        low(inverse_inner),
        low(leave[rows]),
        low(leave),
    )


def dot(a, b):
    return jnp.dot(a, b, preferred_element_type=F32)


def flip(x):
    n = x.shape[1]
    eye = (
        lax.broadcasted_iota(jnp.int32, (n, n), 0) == lax.broadcasted_iota(jnp.int32, (n, n), 1)
    ).astype(BF16)
    return lax.dot_general(
        eye, x, (((1,), (1,)), ((), ())), preferred_element_type=F32
    ).astype(BF16)


def regroup(x, outer, inner):
    n = outer * inner
    row = lax.broadcasted_iota(jnp.int32, (n, n), 0)
    col = lax.broadcasted_iota(jnp.int32, (n, n), 1)
    place = (col == (row % outer) * inner + row // outer).astype(BF16)
    return dot(place, x).astype(BF16)


def mixer_kernel(
    sizes,
    ig_hbm, va_hbm, og_hbm, go_hbm, taps_hbm, entry_nat_hbm, cos_hbm, sin_hbm, fwd_hbm,
    entry_hbm, inv_hbm, leave_hbm, leave_nat_hbm,
    conv_ref, back_ref, filter_ref, skip_ref,
    ig, va, og, go, taps, entry_nat_in, cos, sin, fwd_in, entry_in, inv_in, leave_in,
    leave_nat_in, taps_rows, entry_nat, fwd, entry, inv, leave, leave_nat,
    send1, recv1, send2, recv2, send3, recv3, send4, recv4,
    fsend, frecv, near_sum, near_recv, far_sum, far_recv, dp_sum, dp_recv, kern,
    load_sem, send_sem, recv_sem,
):
    n_dp, far, near, chans, block = sizes
    ctx = far * near
    outer = 2 * ctx
    d = lax.axis_index("dp")
    c = lax.axis_index("context")
    g = c // near
    h = c % near

    pairs = (
        (ig_hbm, ig), (va_hbm, va), (og_hbm, og), (go_hbm, go), (taps_hbm, taps),
        (entry_nat_hbm, entry_nat_in), (cos_hbm, cos), (sin_hbm, sin), (fwd_hbm, fwd_in),
        (entry_hbm, entry_in), (inv_hbm, inv_in), (leave_hbm, leave_in),
        (leave_nat_hbm, leave_nat_in),
    )
    loads = [pltpu.make_async_copy(src, dst, load_sem.at[i]) for i, (src, dst) in enumerate(pairs)]
    for load in loads:
        load.start()

    def far_peer(i):
        t = lax.rem(g + i, far)
        return t, (d, t * near + h)

    def near_peer(i):
        t = lax.rem(h + i, near)
        return t, (d, g * near + t)

    def dp_peer(i):
        t = lax.rem(d + i, n_dp)
        return t, (t, c)

    barrier = pltpu.get_barrier_semaphore()

    def greet(peer):
        def step(i, carry):
            pl.semaphore_signal(barrier, inc=1, device_id=peer(i)[1], device_id_type=MESH)
            return carry

        return step

    lax.fori_loop(1, far, greet(far_peer), 0)
    lax.fori_loop(1, near, greet(near_peer), 0)
    half = n_dp // 2
    ahead = d + (d // half) * (half - 1 - 2 * lax.rem(d, half))

    def send_all(peer, count, src, dst, own, sem):
        def step(i, carry):
            t, target = peer(i)
            pltpu.make_async_remote_copy(
                src_ref=src(t),
                dst_ref=dst.at[own],
                send_sem=send_sem.at[sem],
                recv_sem=recv_sem.at[sem],
                device_id=target,
                device_id_type=MESH,
            ).start()
            return carry

        lax.fori_loop(1, count, step, 0, unroll=UNROLL)

    def wait_blocks(dst, count, sems, i):
        part = dst.at[pl.ds(0, count - 1)]
        pltpu.make_async_copy(part, part, sems.at[i]).wait()

    for i in range(4):
        loads[i].wait()
    mixed = (ig[...].astype(F32) * va[...].astype(F32)).astype(BF16)
    gmix = (go[...].astype(F32) * og[...].astype(F32)).astype(BF16)
    cols = flip(jnp.concatenate([mixed, gmix], 0))
    send1[:, 0] = cols[:, :block].reshape(far, 2 * near, block)
    send1[:, 1] = cols[:, block:].reshape(far, 2 * near, block)
    recv1[g] = send1[g]
    near_sum[...] = jnp.sum(mixed.astype(F32) * gmix.astype(F32), axis=0, keepdims=True)
    near_recv[h] = near_sum[...]

    pl.semaphore_wait(barrier, far + near - 2 + ahead)
    lax.fori_loop(1, n_dp, greet(dp_peer), 0)
    send_all(far_peer, far, lambda t: send1.at[t], recv1, g, 0)
    send_all(near_peer, near, lambda t: near_sum, near_recv, h, 4)

    def forward(table, x):
        section = dot(table, x)
        out = []
        for i in range(x.shape[1] // block):
            re = section[:outer, i * block : (i + 1) * block]
            im = section[outer:, i * block : (i + 1) * block]
            turned = jnp.concatenate(
                [
                    (re * cos[...] + im * sin[...]).astype(BF16),
                    (im * cos[...] - re * sin[...]).astype(BF16),
                ],
                1,
            )
            out.append(dot(turned, fwd[...]))
        return out

    def inverse(table, spectra):
        real, imag = [], []
        for spectrum in spectra:
            back = dot(spectrum, inv[...])
            re, im = back[:, :block], back[:, block:]
            real.append((re * cos[...] - im * sin[...]).astype(BF16))
            imag.append((im * cos[...] + re * sin[...]).astype(BF16))
        turned = jnp.concatenate([jnp.concatenate(real, 1), jnp.concatenate(imag, 1)], 0)
        return dot(table, turned)

    for i in range(4, 9):
        loads[i].wait()
    entry_nat[...] = entry_nat_in[...].astype(BF16)
    fwd[...] = fwd_in[...].astype(BF16)
    for j in range(2):
        for a in range(ctx):
            taps_rows[j, pl.ds(a, 1)] = taps[pl.ds(j, 1), pl.ds(a * block, block)].astype(F32)
    both = jnp.concatenate([taps_rows[0], taps_rows[1]], 1).astype(BF16)
    for j, spectrum in enumerate(forward(entry_nat[...], both)):
        kern[j] = spectrum

    wait_blocks(recv1, far, recv_sem, 0)
    rows = jnp.concatenate(
        [recv1[:, 0].reshape(chans, block), recv1[:, 1].reshape(chans, block)], 1
    )
    rows = regroup(rows, far, 2 * near)
    send2[:, 0] = rows[:, :block].reshape(near, 2, far, block)
    send2[:, 1] = rows[:, block:].reshape(near, 2, far, block)
    recv2[h] = send2[h]
    send_all(near_peer, near, lambda t: send2.at[t], recv2, h, 1)

    def total(blocks, count):
        value = blocks[0]
        for i in range(1, count):
            value = value + blocks[i]
        return value

    wait_blocks(near_recv, near, recv_sem, 4)
    far_sum[...] = total(near_recv, near)
    far_recv[g] = far_sum[...]
    send_all(far_peer, far, lambda t: far_sum, far_recv, g, 7)

    for i in range(9, 13):
        loads[i].wait()
    entry[...] = entry_in[...].astype(BF16)
    inv[...] = inv_in[...].astype(BF16)
    leave[...] = leave_in[...].astype(BF16)
    leave_nat[...] = leave_nat_in[...].astype(BF16)
    wait_blocks(recv2, near, recv_sem, 1)

    sources, gradients = [], []
    for j in range(2):
        halves = [recv2[:, i, j].reshape(ctx, block) for i in range(2)]
        u, v = forward(entry[...], jnp.concatenate(halves, 1))
        sources.append((u[:, :block], u[:, block:]))
        gradients.append((v[:, :block], v[:, block:]))

    specs = []
    for (ur, ui), (vr, vi) in zip(sources, gradients):
        specs.append(jnp.concatenate([ur * vr + ui * vi, ur * vi - ui * vr], 1).astype(BF16))
    term = inverse(leave_nat[...], specs).astype(BF16)
    fsend[:, 0] = term[:, :block].reshape(n_dp, ctx // n_dp, block)
    fsend[:, 1] = term[:, block:].reshape(n_dp, ctx // n_dp, block)
    frecv[d] = fsend[d]

    @pl.when(ahead < n_dp - 1)
    def _():
        pl.semaphore_wait(barrier, n_dp - 1 - ahead)

    send_all(dp_peer, n_dp, lambda t: fsend.at[t], frecv, d, 5)

    for j in range(2):
        (ur, ui), (vr, vi) = sources[j], gradients[j]
        k = kern[j]
        kr, ki = k[:, :block], k[:, block:]
        conv = jnp.concatenate([ur * kr - ui * ki, ur * ki + ui * kr], 1).astype(BF16)
        back = jnp.concatenate([kr * vr + ki * vi, kr * vi - ki * vr], 1).astype(BF16)
        both = inverse(leave[...], [conv, back]).astype(BF16)
        send3[:, 0, j] = both[:, :block].reshape(near, far, block)
        send3[:, 1, j] = both[:, block:].reshape(near, far, block)
    recv3[h] = send3[h]
    send_all(near_peer, near, lambda t: send3.at[t], recv3, h, 3)

    wait_blocks(far_recv, far, recv_sem, 7)
    dp_sum[...] = total(far_recv, far)
    dp_recv[d] = dp_sum[...]
    send_all(dp_peer, n_dp, lambda t: dp_sum, dp_recv, d, 2)

    wait_blocks(recv3, near, recv_sem, 3)
    rows = jnp.concatenate(
        [recv3[:, 0].reshape(chans, block), recv3[:, 1].reshape(chans, block)], 1
    )
    rows = regroup(rows, 2 * near, far)
    send4[:, 0] = rows[:, :block].reshape(far, 2 * near, block)
    send4[:, 1] = rows[:, block:].reshape(far, 2 * near, block)
    recv4[g] = send4[g]
    send_all(far_peer, far, lambda t: send4.at[t], recv4, g, 6)

    wait_blocks(recv4, far, recv_sem, 6)
    tokens = flip(
        jnp.concatenate(
            [recv4[:, 0].reshape(chans, block), recv4[:, 1].reshape(chans, block)], 1
        )
    )
    conv_ref[...] = tokens[:block]
    back_ref[...] = tokens[block:]

    scale = 1.0 / math.sqrt(n_dp * ctx * block)
    wait_blocks(dp_recv, n_dp, recv_sem, 2)
    skip_ref[...] = total(dp_recv, n_dp) * scale
    wait_blocks(frecv, n_dp, recv_sem, 5)
    grad = frecv[0].astype(F32)
    for i in range(1, n_dp):
        grad = grad + frecv[i].astype(F32)
    filter_ref[...] = grad * scale

    wait_blocks(recv1, far, send_sem, 0)
    wait_blocks(recv2, near, send_sem, 1)
    wait_blocks(dp_recv, n_dp, send_sem, 2)
    wait_blocks(recv3, near, send_sem, 3)
    wait_blocks(near_recv, near, send_sem, 4)
    wait_blocks(frecv, n_dp, send_sem, 5)
    wait_blocks(recv4, far, send_sem, 6)
    wait_blocks(far_recv, far, send_sem, 7)


def per_device(input_gate, values, output_gate, grad_out, filter_taps, skip_gain):
    n_dp = lax.axis_size("dp")
    ctx = lax.axis_size("context")
    far, near = group_sizes(ctx)
    block, chans = input_gate.shape[1:]
    rows = np.arange(ctx).reshape(far, near).T.reshape(-1)
    tables = dft_tables(ctx, block, rows, 1.0 / (2 * ctx * block))
    gates = (input_gate[0], values[0], output_gate[0], grad_out[0])
    operands = gates + (filter_taps,) + tables
    share = ctx // n_dp
    outs = (
        jax.ShapeDtypeStruct((block, chans), BF16),
        jax.ShapeDtypeStruct((block, chans), BF16),
        jax.ShapeDtypeStruct((2, share, block), F32),
        jax.ShapeDtypeStruct((1, chans), F32),
    )
    vmem = pltpu.VMEM
    conv_out, conv_back, filter_grad, skip_grad = pl.pallas_call(
        functools.partial(mixer_kernel, (n_dp, far, near, chans, block)),
        out_shape=outs,
        in_specs=[pl.BlockSpec(memory_space=pl.ANY)] * len(operands),
        out_specs=tuple(pl.BlockSpec(memory_space=pltpu.VMEM) for _ in outs),
        scratch_shapes=[vmem(x.shape, x.dtype) for x in operands]
        + [vmem((2, ctx, block), F32)]
        + [vmem(tables[i].shape, BF16) for i in (0, 3, 4, 5, 6, 7)]
        + [vmem((far, 2, 2 * near, block), BF16)] * 2
        + [vmem((near, 2, 2, far, block), BF16)] * 4
        + [vmem((far, 2, 2 * near, block), BF16)] * 2
        + [vmem((n_dp, 2, share, block), BF16)] * 2
        + [vmem((1, chans), F32), vmem((near, 1, chans), F32)]
        + [vmem((1, chans), F32), vmem((far, 1, chans), F32)]
        + [vmem((1, chans), F32), vmem((n_dp, 1, chans), F32)]
        + [vmem((2, 2 * ctx, 2 * block), F32)]
        + [
            pltpu.SemaphoreType.DMA((len(operands),)),
            pltpu.SemaphoreType.DMA((8,)),
            pltpu.SemaphoreType.DMA((8,)),
        ],
        compiler_params=pltpu.CompilerParams(
            collective_id=0, has_side_effects=True, vmem_limit_bytes=64 * 1024 * 1024
        ),
        name="mixer",
    )(*operands)

    gate_in, value, gate_out, cotangent = (x.astype(F32) for x in gates)
    mixed = (gate_in * value).astype(BF16).astype(F32)
    grad_mix = (cotangent * gate_out).astype(BF16).astype(F32)
    grad_output = (cotangent * (conv_out.astype(F32) + skip_gain * mixed)).astype(BF16)
    grad_mixed = conv_back.astype(F32) + skip_gain * grad_mix
    grad_input = (grad_mixed * value).astype(BF16)
    grad_value = (grad_mixed * gate_in).astype(BF16)
    return (
        grad_input[None],
        grad_value[None],
        grad_output[None],
        filter_grad.reshape(2, share * block),
        skip_grad.reshape(-1),
    )


def solution(mesh):
    return jax.shard_map(
        per_device,
        mesh=mesh,
        in_specs=(
            P("dp", "context", None),
            P("dp", "context", None),
            P("dp", "context", None),
            P("dp", "context", None),
            P("context", None),
            P(),
        ),
        out_specs=(
            P("dp", "context", None),
            P("dp", "context", None),
            P("dp", "context", None),
            P("context", "dp"),
            P(),
        ),
        check_vma=False,
    )
```

```python
import functools
import math

import jax
import jax.numpy as jnp
import numpy as np
from jax import lax
from jax.experimental import pallas as pl
from jax.experimental.pallas import tpu as pltpu
from jax.sharding import PartitionSpec as P

MESH = pl.DeviceIdType.MESH
F32 = jnp.float32
BF16 = jnp.bfloat16


def group_sizes(context):
    near = 1
    while 2 * near * near * 2 <= context:
        near *= 2
    return context // near, near


def dft_tables(pieces, block_len, rows, scale):
    outer = 2 * pieces
    total = outer * block_len

    def angle(first, second, modulus):
        return (first[:, None] * second[None, :] % modulus) * (2.0 * math.pi / modulus)

    across = np.arange(pieces)
    outer_index = np.arange(outer)
    inner_index = np.arange(block_len)
    first = angle(outer_index, across, outer)
    entry = np.concatenate([np.cos(first), -np.sin(first)], 0)
    twist = angle(outer_index, inner_index, total)
    twist_cos, twist_sin = np.cos(twist), np.sin(twist)
    inner = angle(inner_index, inner_index, block_len)
    cosine, sine = np.cos(inner), np.sin(inner)
    forward_inner = np.block([[cosine, -sine], [sine, cosine]])
    inverse_inner = np.block([[cosine, sine], [-sine, cosine]])
    last = angle(across, outer_index, outer)
    leave = np.concatenate([np.cos(last), -np.sin(last)], 1) * scale

    def low(table):
        return table.astype(BF16).astype(np.float32)

    return (
        low(entry),
        twist_cos.astype(np.float32),
        twist_sin.astype(np.float32),
        low(forward_inner),
        low(entry[:, rows]),
        low(inverse_inner),
        low(leave[rows]),
        low(leave),
    )


def dot(a, b):
    return jnp.dot(a, b, preferred_element_type=F32)


def flip(x):
    n = x.shape[1]
    eye = (
        lax.broadcasted_iota(jnp.int32, (n, n), 0) == lax.broadcasted_iota(jnp.int32, (n, n), 1)
    ).astype(BF16)
    return lax.dot_general(
        eye, x, (((1,), (1,)), ((), ())), preferred_element_type=F32
    ).astype(BF16)


def regroup(x, outer, inner):
    n = outer * inner
    row = lax.broadcasted_iota(jnp.int32, (n, n), 0)
    col = lax.broadcasted_iota(jnp.int32, (n, n), 1)
    place = (col == (row % outer) * inner + row // outer).astype(BF16)
    return dot(place, x).astype(BF16)


def mixer_kernel(
    sizes,
    ig_hbm, va_hbm, og_hbm, go_hbm, gain_hbm, taps_hbm, entry_nat_hbm, cos_hbm, sin_hbm, fwd_hbm,
    entry_hbm, inv_hbm, leave_hbm, leave_nat_hbm,
    gin_hbm, gval_hbm, gout_hbm, filter_hbm, skip_hbm,
    ig, va, og, go, gain, taps, entry_nat_in, cos, sin, fwd_in, entry_in, inv_in, leave_in,
    leave_nat_in, taps_rows, entry_nat, fwd, entry, inv, leave, leave_nat,
    gin, gval, gout, filter_out, skip_out,
    send1, recv1, send2, recv2, send3, recv3, send4, recv4,
    near_sum, near_recv, far_sum, far_recv, fsend, frecv, dp_sum, dp_recv, kern,
    load_sem, store_sem, send_sem, recv_sem, fsend_sem, frecv_sem, dsend_sem, drecv_sem,
):
    n_dp, far, near, chans, block = sizes
    ctx = far * near
    outer = 2 * ctx
    d = lax.axis_index("dp")
    c = lax.axis_index("context")
    g = c // near
    h = c % near

    pairs = (
        (ig_hbm, ig), (va_hbm, va), (og_hbm, og), (go_hbm, go), (taps_hbm, taps),
        (entry_nat_hbm, entry_nat_in), (cos_hbm, cos), (sin_hbm, sin), (fwd_hbm, fwd_in),
        (entry_hbm, entry_in), (inv_hbm, inv_in), (leave_hbm, leave_in),
        (leave_nat_hbm, leave_nat_in), (gain_hbm, gain),
    )
    loads = [pltpu.make_async_copy(src, dst, load_sem.at[i]) for i, (src, dst) in enumerate(pairs)]
    for load in loads[:4]:
        load.start()

    def far_peer(i):
        t = lax.rem(g + i, far)
        return t, (d, t * near + h)

    def near_peer(i):
        t = lax.rem(h + i, near)
        return t, (d, g * near + t)

    barrier = pltpu.get_barrier_semaphore()

    def greet(peer):
        def step(i, carry):
            pl.semaphore_signal(barrier, inc=1, device_id=peer(i)[1], device_id_type=MESH)
            return carry

        return step

    half = n_dp // 2

    def order(t):
        return t + (t // half) * (half - 1 - 2 * lax.rem(t, half))

    ahead = order(d)
    others = [lax.rem(d + i, n_dp) for i in range(1, n_dp)]
    lax.fori_loop(1, far, greet(far_peer), 0)
    lax.fori_loop(1, near, greet(near_peer), 0)
    for t in others:

        @pl.when(order(t) > ahead)
        def _():
            pl.semaphore_signal(barrier, inc=1, device_id=(t, c), device_id_type=MESH)

    for load in loads[4:]:
        load.start()

    def send_all(peer, count, src, dst, own, sem):
        def step(i, carry):
            t, target = peer(i)
            pltpu.make_async_remote_copy(
                src_ref=src(t),
                dst_ref=dst.at[own],
                send_sem=send_sem.at[sem],
                recv_sem=recv_sem.at[sem],
                device_id=target,
                device_id_type=MESH,
            ).start()
            return carry

        lax.fori_loop(1, count, step, 0)

    def wait_blocks(dst, count, sems, i):
        part = dst.at[pl.ds(0, count - 1)]
        pltpu.make_async_copy(part, part, sems.at[i]).wait()

    def wait_one(ref, sem):
        pltpu.make_async_copy(ref, ref, sem).wait()

    def total(blocks, count):
        value = blocks[0]
        for i in range(1, count):
            value = value + blocks[i]
        return value

    def product(a, b):
        return (a[...].astype(F32) * b[...].astype(F32)).astype(BF16)

    for i in range(4):
        loads[i].wait()
    mixed, gmix = product(ig, va), product(go, og)
    for i, tokens in enumerate((mixed, gmix)):
        send1[i] = flip(tokens).reshape(far, 2 * near, block)
        recv1[i, g] = send1[i, g]
    near_sum[...] = jnp.sum(mixed.astype(F32) * gmix.astype(F32), axis=0, keepdims=True)
    near_recv[h] = near_sum[...]

    pl.semaphore_wait(barrier, far + near - 2 + ahead)
    for i in range(2):
        send_all(far_peer, far, lambda t: send1.at[i, t], recv1.at[i], g, i)
    send_all(near_peer, near, lambda t: near_sum, near_recv, h, 8)

    def forward(table, x):
        section = dot(table, x)
        out = []
        for i in range(x.shape[1] // block):
            re = section[:outer, i * block : (i + 1) * block]
            im = section[outer:, i * block : (i + 1) * block]
            turned = jnp.concatenate(
                [
                    (re * cos[...] + im * sin[...]).astype(BF16),
                    (im * cos[...] - re * sin[...]).astype(BF16),
                ],
                1,
            )
            out.append(dot(turned, fwd[...]))
        return out

    def inverse(table, spectra):
        real, imag = [], []
        for spectrum in spectra:
            back = dot(spectrum, inv[...])
            re, im = back[:, :block], back[:, block:]
            real.append((re * cos[...] - im * sin[...]).astype(BF16))
            imag.append((im * cos[...] + re * sin[...]).astype(BF16))
        turned = jnp.concatenate([jnp.concatenate(real, 1), jnp.concatenate(imag, 1)], 0)
        return dot(table, turned).astype(BF16)

    for i in range(4, 14):
        loads[i].wait()
    entry_nat[...] = entry_nat_in[...].astype(BF16)
    fwd[...] = fwd_in[...].astype(BF16)
    for j in range(2):
        for a in range(ctx):
            taps_rows[j, pl.ds(a, 1)] = taps[pl.ds(j, 1), pl.ds(a * block, block)].astype(F32)
    both = jnp.concatenate([taps_rows[0], taps_rows[1]], 1).astype(BF16)
    for j, spectrum in enumerate(forward(entry_nat[...], both)):
        kern[j] = spectrum
    entry[...] = entry_in[...].astype(BF16)
    inv[...] = inv_in[...].astype(BF16)
    leave[...] = leave_in[...].astype(BF16)
    leave_nat[...] = leave_nat_in[...].astype(BF16)

    for i in range(2):
        wait_blocks(recv1.at[i], far, recv_sem, i)
        rows = regroup(recv1[i].reshape(chans, block), far, 2 * near)
        send2[i] = rows.reshape(near, 2, far, block)
        recv2[i, h] = send2[i, h]
        send_all(near_peer, near, lambda t: send2.at[i, t], recv2.at[i], h, 2 + i)

    wait_blocks(near_recv, near, recv_sem, 8)
    far_sum[...] = total(near_recv, near)
    far_recv[g] = far_sum[...]
    send_all(far_peer, far, lambda t: far_sum, far_recv, g, 9)

    spectra = []
    for i in range(2):
        wait_blocks(recv2.at[i], near, recv_sem, 2 + i)
        both = jnp.concatenate([recv2[i, :, j].reshape(ctx, block) for j in range(2)], 1)
        spectra.append([(s[:, :block], s[:, block:]) for s in forward(entry[...], both)])
    sources, gradients = spectra

    specs = []
    for (ur, ui), (vr, vi) in zip(sources, gradients):
        specs.append(jnp.concatenate([ur * vr + ui * vi, ur * vi - ui * vr], 1).astype(BF16))
    term = inverse(leave_nat[...], specs)
    for j in range(2):
        part = term[:, j * block : (j + 1) * block]
        fsend[:, j] = part.reshape(n_dp, ctx // n_dp, block)
    frecv[d] = fsend[d]
    wait_blocks(far_recv, far, recv_sem, 9)
    dp_sum[...] = total(far_recv, far)
    dp_recv[d] = dp_sum[...]

    def send_shares(t):
        for src, dst, out, come in (
            (fsend.at[t], frecv.at[d], fsend_sem.at[t], frecv_sem.at[d]),
            (dp_sum, dp_recv.at[d], dsend_sem.at[t], drecv_sem.at[d]),
        ):
            pltpu.make_async_remote_copy(
                src_ref=src,
                dst_ref=dst,
                send_sem=out,
                recv_sem=come,
                device_id=(t, c),
                device_id_type=MESH,
            ).start()

    for t in others:

        @pl.when(order(t) < ahead)
        def _():
            send_shares(t)

    kernels = [(kern[j][:, :block], kern[j][:, block:]) for j in range(2)]
    convs, backs = [], []
    for (ur, ui), (vr, vi), (kr, ki) in zip(sources, gradients, kernels):
        convs.append(jnp.concatenate([ur * kr - ui * ki, ur * ki + ui * kr], 1).astype(BF16))
        backs.append(jnp.concatenate([kr * vr + ki * vi, kr * vi - ki * vr], 1).astype(BF16))
    for i, specs in enumerate((convs, backs)):
        both = inverse(leave[...], specs)
        for j in range(2):
            part = both[:, j * block : (j + 1) * block]
            send3[i, :, j] = part.reshape(near, far, block)
        recv3[i, h] = send3[i, h]
        send_all(near_peer, near, lambda t: send3.at[i, t], recv3.at[i], h, 4 + i)

    for i in range(2):
        wait_blocks(recv3.at[i], near, recv_sem, 4 + i)
        rows = regroup(recv3[i].reshape(chans, block), 2 * near, far)
        send4[i] = rows.reshape(far, 2 * near, block)
        recv4[i, g] = send4[i, g]
        send_all(far_peer, far, lambda t: send4.at[i, t], recv4.at[i], g, 6 + i)

    stores = [
        pltpu.make_async_copy(src, dst, store_sem.at[i])
        for i, (src, dst) in enumerate(
            (
                (gout, gout_hbm), (gin, gin_hbm), (gval, gval_hbm),
                (skip_out, skip_hbm), (filter_out, filter_hbm),
            )
        )
    ]
    wait_blocks(recv4.at[0], far, recv_sem, 6)
    conv = flip(recv4[0].reshape(chans, block)).astype(F32)
    gains = gain[...]
    gout[...] = (
        go[...].astype(F32) * (conv + gains * product(ig, va).astype(F32))
    ).astype(BF16)
    stores[0].start()
    wait_blocks(recv4.at[1], far, recv_sem, 7)
    back = flip(recv4[1].reshape(chans, block)).astype(F32)
    grad_mixed = back + gains * product(go, og).astype(F32)
    gin[...] = (grad_mixed * va[...].astype(F32)).astype(BF16)
    gval[...] = (grad_mixed * ig[...].astype(F32)).astype(BF16)
    stores[1].start()
    stores[2].start()

    for t in others:

        @pl.when(order(t) > ahead)
        def _():
            wait_one(frecv.at[t], frecv_sem.at[t])
            send_shares(t)

    for t in others:

        @pl.when(order(t) < ahead)
        def _():
            wait_one(frecv.at[t], frecv_sem.at[t])

    scale = 1.0 / math.sqrt(n_dp * ctx * block)
    grad = frecv[0].astype(F32)
    for i in range(1, n_dp):
        grad = grad + frecv[i].astype(F32)
    grad = grad * scale
    for j in range(2):
        for a in range(ctx // n_dp):
            filter_out[pl.ds(j, 1), pl.ds(a * block, block)] = grad[j, a : a + 1]
    stores[4].start()
    for t in others:
        wait_one(dp_recv.at[t], drecv_sem.at[t])
    skip_out[...] = total(dp_recv, n_dp) * scale
    stores[3].start()

    for i in range(2):
        wait_blocks(recv1.at[i], far, send_sem, i)
        wait_blocks(recv2.at[i], near, send_sem, 2 + i)
        wait_blocks(recv3.at[i], near, send_sem, 4 + i)
        wait_blocks(recv4.at[i], far, send_sem, 6 + i)
    wait_blocks(near_recv, near, send_sem, 8)
    wait_blocks(far_recv, far, send_sem, 9)
    for t in others:
        wait_one(fsend.at[t], fsend_sem.at[t])
        wait_one(dp_sum, dsend_sem.at[t])
    for store in stores:
        store.wait()


def copy_kernel(*refs):
    n = (len(refs) - 1) // 2
    copies = [pltpu.make_async_copy(refs[i], refs[n + i], refs[-1].at[i]) for i in range(n)]
    for copy in copies:
        copy.start()
    for copy in copies:
        copy.wait()


def per_device(input_gate, values, output_gate, grad_out, filter_taps, skip_gain):
    n_dp = lax.axis_size("dp")
    ctx = lax.axis_size("context")
    far, near = group_sizes(ctx)
    block, chans = input_gate.shape[1:]
    rows = np.arange(ctx).reshape(far, near).T.reshape(-1)
    tables = dft_tables(ctx, block, rows, 1.0 / (2 * ctx * block))
    gates = (input_gate[0], values[0], output_gate[0], grad_out[0], skip_gain.reshape(1, -1))
    operands = gates + (filter_taps,) + tables
    share = ctx // n_dp
    outs = tuple(jax.ShapeDtypeStruct((block, chans), BF16) for _ in range(3)) + (
        jax.ShapeDtypeStruct((2, share * block), F32),
        jax.ShapeDtypeStruct((1, chans), F32),
    )
    vmem = pltpu.VMEM
    dma = pltpu.SemaphoreType.DMA
    results = pl.pallas_call(
        functools.partial(mixer_kernel, (n_dp, far, near, chans, block)),
        out_shape=outs,
        in_specs=[pl.BlockSpec(memory_space=pl.ANY)] * len(operands),
        out_specs=tuple(pl.BlockSpec(memory_space=pl.ANY) for _ in outs),
        scratch_shapes=[vmem(x.shape, x.dtype) for x in operands]
        + [vmem((2, ctx, block), F32)]
        + [vmem(tables[i].shape, BF16) for i in (0, 3, 4, 5, 6, 7)]
        + [vmem(x.shape, x.dtype) for x in outs]
        + [vmem((2, far, 2 * near, block), BF16)] * 2
        + [vmem((2, near, 2, far, block), BF16)] * 4
        + [vmem((2, far, 2 * near, block), BF16)] * 2
        + [vmem((1, chans), F32), vmem((near, 1, chans), F32)]
        + [vmem((1, chans), F32), vmem((far, 1, chans), F32)]
        + [vmem((n_dp, 2, share, block), BF16)] * 2
        + [vmem((1, chans), F32), vmem((n_dp, 1, chans), F32)]
        + [vmem((2, 2 * ctx, 2 * block), F32)]
        + [dma((len(operands),)), dma((len(outs),)), dma((10,)), dma((10,))]
        + [dma((n_dp,))] * 4,
        compiler_params=pltpu.CompilerParams(
            collective_id=0, has_side_effects=True, vmem_limit_bytes=64 * 1024 * 1024
        ),
        name="mixer",
    )(*operands)
    grad_input, grad_value, grad_output, filter_grad, skip_grad = pl.pallas_call(
        copy_kernel,
        out_shape=outs,
        in_specs=[pl.BlockSpec(memory_space=pl.ANY)] * len(outs),
        out_specs=tuple(pl.BlockSpec(memory_space=pl.ANY) for _ in outs),
        scratch_shapes=[dma((len(outs),))],
        compiler_params=pltpu.CompilerParams(vmem_limit_bytes=64 * 1024 * 1024),
        name="results",
    )(*results)
    return (
        grad_input[None],
        grad_value[None],
        grad_output[None],
        filter_grad,
        skip_grad.reshape(-1),
    )


def solution(mesh):
    return jax.shard_map(
        per_device,
        mesh=mesh,
        in_specs=(
            P("dp", "context", None),
            P("dp", "context", None),
            P("dp", "context", None),
            P("dp", "context", None),
            P("context", None),
            P(),
        ),
        out_specs=(
            P("dp", "context", None),
            P("dp", "context", None),
            P("dp", "context", None),
            P("context", "dp"),
            P(),
        ),
        check_vma=False,
    )
```

```python
import functools
import math

import jax
import jax.numpy as jnp
import numpy as np
from jax import lax
from jax.experimental import pallas as pl
from jax.experimental.pallas import tpu as pltpu
from jax.sharding import PartitionSpec as P

MESH = pl.DeviceIdType.MESH
F32 = jnp.float32
BF16 = jnp.bfloat16


def group_sizes(context):
    near = 1
    while 2 * near * near * 2 <= context:
        near *= 2
    return context // near, near


def dft_tables(pieces, block_len, rows, scale):
    outer = 2 * pieces
    total = outer * block_len

    def angle(first, second, modulus):
        return (first[:, None] * second[None, :] % modulus) * (2.0 * math.pi / modulus)

    across = np.arange(pieces)
    outer_index = np.arange(outer)
    inner_index = np.arange(block_len)
    first = angle(outer_index, across, outer)
    entry = np.concatenate([np.cos(first), -np.sin(first)], 0)
    twist = angle(outer_index, inner_index, total)
    twist_cos, twist_sin = np.cos(twist), np.sin(twist)
    inner = angle(inner_index, inner_index, block_len)
    cosine, sine = np.cos(inner), np.sin(inner)
    forward_inner = np.block([[cosine, -sine], [sine, cosine]])
    inverse_inner = np.block([[cosine, sine], [-sine, cosine]])
    last = angle(across, outer_index, outer)
    leave = np.concatenate([np.cos(last), -np.sin(last)], 1) * scale

    def low(table):
        return table.astype(BF16).astype(np.float32)

    return (
        low(entry),
        twist_cos.astype(np.float32),
        twist_sin.astype(np.float32),
        low(forward_inner),
        low(entry[:, rows]),
        low(inverse_inner),
        low(leave[rows]),
        low(leave),
    )


def dot(a, b):
    return jnp.dot(a, b, preferred_element_type=F32)


def flip(x):
    n = x.shape[1]
    eye = (
        lax.broadcasted_iota(jnp.int32, (n, n), 0) == lax.broadcasted_iota(jnp.int32, (n, n), 1)
    ).astype(BF16)
    return lax.dot_general(
        eye, x, (((1,), (1,)), ((), ())), preferred_element_type=F32
    ).astype(BF16)


def regroup(x, outer, inner):
    n = outer * inner
    row = lax.broadcasted_iota(jnp.int32, (n, n), 0)
    col = lax.broadcasted_iota(jnp.int32, (n, n), 1)
    place = (col == (row % outer) * inner + row // outer).astype(BF16)
    return dot(place, x).astype(BF16)


def mixer_kernel(
    sizes,
    ig_hbm, va_hbm, og_hbm, go_hbm, gain_hbm, taps_hbm, entry_nat_hbm, cos_hbm, sin_hbm, fwd_hbm,
    entry_hbm, inv_hbm, leave_hbm, leave_nat_hbm,
    gin_hbm, gval_hbm, gout_hbm, filter_hbm, skip_hbm,
    ig, va, og, go, gain, taps, entry_nat_in, cos, sin, fwd_in, entry_in, inv_in, leave_in,
    leave_nat_in, taps_rows, entry_nat, fwd, entry, inv, leave, leave_nat,
    gin, gval, gout, filter_out, skip_out,
    send1, recv1, send2, recv2, send3, recv3, send4, recv4,
    near_sum, near_recv, far_sum, far_recv, fsend, frecv, dp_sum, dp_recv, word, words, kern,
    load_sem, store_sem, send_sem, recv_sem, fsend_sem, frecv_sem, dsend_sem, drecv_sem,
    wsend_sem, wrecv_sem,
):
    n_dp, far, near, chans, block = sizes
    ctx = far * near
    outer = 2 * ctx
    d = lax.axis_index("dp")
    c = lax.axis_index("context")
    g = c // near
    h = c % near

    pairs = (
        (ig_hbm, ig), (va_hbm, va), (og_hbm, og), (go_hbm, go), (taps_hbm, taps),
        (entry_nat_hbm, entry_nat_in), (cos_hbm, cos), (sin_hbm, sin), (fwd_hbm, fwd_in),
        (entry_hbm, entry_in), (inv_hbm, inv_in), (leave_hbm, leave_in),
        (leave_nat_hbm, leave_nat_in), (gain_hbm, gain),
    )
    loads = [pltpu.make_async_copy(src, dst, load_sem.at[i]) for i, (src, dst) in enumerate(pairs)]
    for load in loads[:4]:
        load.start()

    def far_peer(i):
        t = lax.rem(g + i, far)
        return t, (d, t * near + h)

    def near_peer(i):
        t = lax.rem(h + i, near)
        return t, (d, g * near + t)

    barrier = pltpu.get_barrier_semaphore()

    def greet(peer):
        def step(i, carry):
            pl.semaphore_signal(barrier, inc=1, device_id=peer(i)[1], device_id_type=MESH)
            return carry

        return step

    half = n_dp // 2

    def order(t):
        return t + (t // half) * (half - 1 - 2 * lax.rem(t, half))

    ahead = order(d)
    others = [lax.rem(d + n_dp - i, n_dp) for i in (2, 1, 3)[: n_dp - 1]] if n_dp > 2 else [1 - d]
    lax.fori_loop(1, far, greet(far_peer), 0)
    lax.fori_loop(1, near, greet(near_peer), 0)
    for t in others:

        @pl.when(order(t) > ahead)
        def _():
            pl.semaphore_signal(barrier, inc=1, device_id=(t, c), device_id_type=MESH)

    for load in loads[4:]:
        load.start()

    def send_all(peer, count, src, dst, own, sem):
        def step(i, carry):
            t, target = peer(i)
            pltpu.make_async_remote_copy(
                src_ref=src(t),
                dst_ref=dst.at[own],
                send_sem=send_sem.at[sem],
                recv_sem=recv_sem.at[sem],
                device_id=target,
                device_id_type=MESH,
            ).start()
            return carry

        lax.fori_loop(1, count, step, 0)

    def wait_blocks(dst, count, sems, i):
        part = dst.at[pl.ds(0, count - 1)]
        pltpu.make_async_copy(part, part, sems.at[i]).wait()

    def wait_one(ref, sem):
        pltpu.make_async_copy(ref, ref, sem).wait()

    def total(blocks, count):
        value = blocks[0]
        for i in range(1, count):
            value = value + blocks[i]
        return value

    def product(a, b):
        return (a[...].astype(F32) * b[...].astype(F32)).astype(BF16)

    for i in range(4):
        loads[i].wait()
    mixed, gmix = product(ig, va), product(go, og)
    for i, tokens in enumerate((mixed, gmix)):
        send1[i] = flip(tokens).reshape(far, 2 * near, block)
        recv1[i, g] = send1[i, g]
    near_sum[...] = jnp.sum(mixed.astype(F32) * gmix.astype(F32), axis=0, keepdims=True)
    near_recv[h] = near_sum[...]
    word[...] = jnp.zeros(word.shape, F32)

    pl.semaphore_wait(barrier, far + near - 2 + ahead)
    for i in range(2):
        send_all(far_peer, far, lambda t: send1.at[i, t], recv1.at[i], g, i)
    send_all(near_peer, near, lambda t: near_sum, near_recv, h, 8)
    for t in others:

        @pl.when(order(t) < ahead)
        def _():
            pltpu.make_async_remote_copy(
                src_ref=word,
                dst_ref=words.at[d],
                send_sem=wsend_sem.at[t],
                recv_sem=wrecv_sem.at[d],
                device_id=(t, c),
                device_id_type=MESH,
            ).start()

    def forward(table, x):
        section = dot(table, x)
        out = []
        for i in range(x.shape[1] // block):
            re = section[:outer, i * block : (i + 1) * block]
            im = section[outer:, i * block : (i + 1) * block]
            turned = jnp.concatenate(
                [
                    (re * cos[...] + im * sin[...]).astype(BF16),
                    (im * cos[...] - re * sin[...]).astype(BF16),
                ],
                1,
            )
            out.append(dot(turned, fwd[...]))
        return out

    def inverse(table, spectra):
        real, imag = [], []
        for spectrum in spectra:
            back = dot(spectrum, inv[...])
            re, im = back[:, :block], back[:, block:]
            real.append((re * cos[...] - im * sin[...]).astype(BF16))
            imag.append((im * cos[...] + re * sin[...]).astype(BF16))
        turned = jnp.concatenate([jnp.concatenate(real, 1), jnp.concatenate(imag, 1)], 0)
        return dot(table, turned).astype(BF16)

    for i in range(4, 14):
        loads[i].wait()
    entry_nat[...] = entry_nat_in[...].astype(BF16)
    fwd[...] = fwd_in[...].astype(BF16)
    for j in range(2):
        for a in range(ctx):
            taps_rows[j, pl.ds(a, 1)] = taps[pl.ds(j, 1), pl.ds(a * block, block)].astype(F32)
    both = jnp.concatenate([taps_rows[0], taps_rows[1]], 1).astype(BF16)
    for j, spectrum in enumerate(forward(entry_nat[...], both)):
        kern[j] = spectrum
    entry[...] = entry_in[...].astype(BF16)
    inv[...] = inv_in[...].astype(BF16)
    leave[...] = leave_in[...].astype(BF16)
    leave_nat[...] = leave_nat_in[...].astype(BF16)

    for i in range(2):
        wait_blocks(recv1.at[i], far, recv_sem, i)
        rows = regroup(recv1[i].reshape(chans, block), far, 2 * near)
        send2[i] = rows.reshape(near, 2, far, block)
        recv2[i, h] = send2[i, h]
        send_all(near_peer, near, lambda t: send2.at[i, t], recv2.at[i], h, 2 + i)

    wait_blocks(near_recv, near, recv_sem, 8)
    far_sum[...] = total(near_recv, near)
    far_recv[g] = far_sum[...]
    send_all(far_peer, far, lambda t: far_sum, far_recv, g, 9)

    spectra = []
    for i in range(2):
        wait_blocks(recv2.at[i], near, recv_sem, 2 + i)
        both = jnp.concatenate([recv2[i, :, j].reshape(ctx, block) for j in range(2)], 1)
        spectra.append([(s[:, :block], s[:, block:]) for s in forward(entry[...], both)])
    sources, gradients = spectra

    specs = []
    for (ur, ui), (vr, vi) in zip(sources, gradients):
        specs.append(jnp.concatenate([ur * vr + ui * vi, ur * vi - ui * vr], 1).astype(BF16))
    term = inverse(leave_nat[...], specs)
    for j in range(2):
        part = term[:, j * block : (j + 1) * block]
        fsend[:, j] = part.reshape(n_dp, ctx // n_dp, block)
    frecv[d] = fsend[d]
    wait_blocks(far_recv, far, recv_sem, 9)
    dp_sum[...] = total(far_recv, far)
    dp_recv[d] = dp_sum[...]

    def send_shares(t):
        for src, dst, out, come in (
            (fsend.at[t], frecv.at[d], fsend_sem.at[t], frecv_sem.at[d]),
            (dp_sum, dp_recv.at[d], dsend_sem.at[t], drecv_sem.at[d]),
        ):
            pltpu.make_async_remote_copy(
                src_ref=src,
                dst_ref=dst,
                send_sem=out,
                recv_sem=come,
                device_id=(t, c),
                device_id_type=MESH,
            ).start()

    for t in others:

        @pl.when(order(t) < ahead)
        def _():
            send_shares(t)

    kernels = [(kern[j][:, :block], kern[j][:, block:]) for j in range(2)]
    convs, backs = [], []
    for (ur, ui), (vr, vi), (kr, ki) in zip(sources, gradients, kernels):
        convs.append(jnp.concatenate([ur * kr - ui * ki, ur * ki + ui * kr], 1).astype(BF16))
        backs.append(jnp.concatenate([kr * vr + ki * vi, kr * vi - ki * vr], 1).astype(BF16))
    for i, specs in enumerate((convs, backs)):
        both = inverse(leave[...], specs)
        for j in range(2):
            part = both[:, j * block : (j + 1) * block]
            send3[i, :, j] = part.reshape(near, far, block)
        recv3[i, h] = send3[i, h]
        send_all(near_peer, near, lambda t: send3.at[i, t], recv3.at[i], h, 4 + i)

    for t in others:

        @pl.when(order(t) > ahead)
        def _():
            wait_one(words.at[t], wrecv_sem.at[t])
            send_shares(t)

    for i in range(2):
        wait_blocks(recv3.at[i], near, recv_sem, 4 + i)
        rows = regroup(recv3[i].reshape(chans, block), 2 * near, far)
        send4[i] = rows.reshape(far, 2 * near, block)
        recv4[i, g] = send4[i, g]
        send_all(far_peer, far, lambda t: send4.at[i, t], recv4.at[i], g, 6 + i)

    stores = [
        pltpu.make_async_copy(src, dst, store_sem.at[i])
        for i, (src, dst) in enumerate(
            (
                (gout, gout_hbm), (gin, gin_hbm), (gval, gval_hbm),
                (skip_out, skip_hbm), (filter_out, filter_hbm),
            )
        )
    ]
    wait_blocks(recv4.at[0], far, recv_sem, 6)
    conv = flip(recv4[0].reshape(chans, block)).astype(F32)
    gains = gain[...]
    gout[...] = (
        go[...].astype(F32) * (conv + gains * product(ig, va).astype(F32))
    ).astype(BF16)
    stores[0].start()
    wait_blocks(recv4.at[1], far, recv_sem, 7)
    back = flip(recv4[1].reshape(chans, block)).astype(F32)
    grad_mixed = back + gains * product(go, og).astype(F32)
    gin[...] = (grad_mixed * va[...].astype(F32)).astype(BF16)
    gval[...] = (grad_mixed * ig[...].astype(F32)).astype(BF16)
    stores[1].start()
    stores[2].start()

    for t in others:
        wait_one(frecv.at[t], frecv_sem.at[t])
    scale = 1.0 / math.sqrt(n_dp * ctx * block)
    grad = frecv[0].astype(F32)
    for i in range(1, n_dp):
        grad = grad + frecv[i].astype(F32)
    grad = grad * scale
    for j in range(2):
        for a in range(ctx // n_dp):
            filter_out[pl.ds(j, 1), pl.ds(a * block, block)] = grad[j, a : a + 1]
    stores[4].start()
    for t in others:
        wait_one(dp_recv.at[t], drecv_sem.at[t])
    skip_out[...] = total(dp_recv, n_dp) * scale
    stores[3].start()

    for i in range(2):
        wait_blocks(recv1.at[i], far, send_sem, i)
        wait_blocks(recv2.at[i], near, send_sem, 2 + i)
        wait_blocks(recv3.at[i], near, send_sem, 4 + i)
        wait_blocks(recv4.at[i], far, send_sem, 6 + i)
    wait_blocks(near_recv, near, send_sem, 8)
    wait_blocks(far_recv, far, send_sem, 9)
    for t in others:
        wait_one(fsend.at[t], fsend_sem.at[t])
        wait_one(dp_sum, dsend_sem.at[t])

        @pl.when(order(t) < ahead)
        def _():
            wait_one(word, wsend_sem.at[t])

    for store in stores:
        store.wait()


def copy_kernel(*refs):
    n = (len(refs) - 2) // 3
    sources, targets, held = refs[:n], refs[n : 2 * n], refs[2 * n : 3 * n]
    come, gone = refs[3 * n :]
    loads = [pltpu.make_async_copy(sources[i], held[i], come.at[i]) for i in range(n)]
    stores = [pltpu.make_async_copy(held[i], targets[i], gone.at[i]) for i in range(n)]
    for load in loads:
        load.start()
    for load, store in zip(loads, stores):
        load.wait()
        store.start()
    for store in stores:
        store.wait()


def per_device(input_gate, values, output_gate, grad_out, filter_taps, skip_gain):
    n_dp = lax.axis_size("dp")
    ctx = lax.axis_size("context")
    far, near = group_sizes(ctx)
    block, chans = input_gate.shape[1:]
    rows = np.arange(ctx).reshape(far, near).T.reshape(-1)
    tables = dft_tables(ctx, block, rows, 1.0 / (2 * ctx * block))
    gates = (input_gate[0], values[0], output_gate[0], grad_out[0], skip_gain.reshape(1, -1))
    operands = gates + (filter_taps,) + tables
    share = ctx // n_dp
    outs = tuple(jax.ShapeDtypeStruct((block, chans), BF16) for _ in range(3)) + (
        jax.ShapeDtypeStruct((2, share * block), F32),
        jax.ShapeDtypeStruct((1, chans), F32),
    )
    vmem = pltpu.VMEM
    dma = pltpu.SemaphoreType.DMA
    results = pl.pallas_call(
        functools.partial(mixer_kernel, (n_dp, far, near, chans, block)),
        out_shape=outs,
        in_specs=[pl.BlockSpec(memory_space=pl.ANY)] * len(operands),
        out_specs=tuple(pl.BlockSpec(memory_space=pl.ANY) for _ in outs),
        scratch_shapes=[vmem(x.shape, x.dtype) for x in operands]
        + [vmem((2, ctx, block), F32)]
        + [vmem(tables[i].shape, BF16) for i in (0, 3, 4, 5, 6, 7)]
        + [vmem(x.shape, x.dtype) for x in outs]
        + [vmem((2, far, 2 * near, block), BF16)] * 2
        + [vmem((2, near, 2, far, block), BF16)] * 4
        + [vmem((2, far, 2 * near, block), BF16)] * 2
        + [vmem((1, chans), F32), vmem((near, 1, chans), F32)]
        + [vmem((1, chans), F32), vmem((far, 1, chans), F32)]
        + [vmem((n_dp, 2, share, block), BF16)] * 2
        + [vmem((1, chans), F32), vmem((n_dp, 1, chans), F32)]
        + [vmem((1, 128), F32), vmem((n_dp, 1, 128), F32)]
        + [vmem((2, 2 * ctx, 2 * block), F32)]
        + [dma((len(operands),)), dma((len(outs),)), dma((10,)), dma((10,))]
        + [dma((n_dp,))] * 6,
        compiler_params=pltpu.CompilerParams(
            collective_id=0, has_side_effects=True, vmem_limit_bytes=64 * 1024 * 1024
        ),
        name="mixer",
    )(*operands)
    grad_input, grad_value, grad_output, filter_grad, skip_grad = pl.pallas_call(
        copy_kernel,
        out_shape=outs,
        in_specs=[pl.BlockSpec(memory_space=pl.ANY)] * len(outs),
        out_specs=tuple(pl.BlockSpec(memory_space=pl.ANY) for _ in outs),
        scratch_shapes=[vmem(x.shape, x.dtype) for x in outs] + [dma((len(outs),))] * 2,
        compiler_params=pltpu.CompilerParams(vmem_limit_bytes=64 * 1024 * 1024),
        name="results",
    )(*results)
    return (
        grad_input[None],
        grad_value[None],
        grad_output[None],
        filter_grad,
        skip_grad.reshape(-1),
    )


def solution(mesh):
    return jax.shard_map(
        per_device,
        mesh=mesh,
        in_specs=(
            P("dp", "context", None),
            P("dp", "context", None),
            P("dp", "context", None),
            P("dp", "context", None),
            P("context", None),
            P(),
        ),
        out_specs=(
            P("dp", "context", None),
            P("dp", "context", None),
            P("dp", "context", None),
            P("context", "dp"),
            P(),
        ),
        check_vma=False,
    )
```

```python
import functools
import math

import jax
import jax.numpy as jnp
import numpy as np
from jax import lax
from jax.experimental import pallas as pl
from jax.experimental.pallas import tpu as pltpu
from jax.sharding import PartitionSpec as P

MESH = pl.DeviceIdType.MESH
F32 = jnp.float32
BF16 = jnp.bfloat16


def group_sizes(context):
    near = 1
    while 2 * near * near * 2 <= context:
        near *= 2
    return context // near, near


def dft_tables(pieces, block_len, rows, scale):
    outer = 2 * pieces
    total = outer * block_len

    def angle(first, second, modulus):
        return (first[:, None] * second[None, :] % modulus) * (2.0 * math.pi / modulus)

    across = np.arange(pieces)
    outer_index = np.arange(outer)
    inner_index = np.arange(block_len)
    first = angle(outer_index, across, outer)
    entry = np.concatenate([np.cos(first), -np.sin(first)], 0)
    twist = angle(outer_index, inner_index, total)
    twist_cos, twist_sin = np.cos(twist), np.sin(twist)
    inner = angle(inner_index, inner_index, block_len)
    cosine, sine = np.cos(inner), np.sin(inner)
    forward_inner = np.block([[cosine, -sine], [sine, cosine]])
    inverse_inner = np.block([[cosine, sine], [-sine, cosine]])
    last = angle(across, outer_index, outer)
    leave = np.concatenate([np.cos(last), -np.sin(last)], 1) * scale

    def low(table):
        return table.astype(BF16).astype(np.float32)

    return (
        low(entry),
        twist_cos.astype(np.float32),
        twist_sin.astype(np.float32),
        low(forward_inner),
        low(entry[:, rows]),
        low(inverse_inner),
        low(leave[rows]),
        low(leave),
    )


def dot(a, b):
    return jnp.dot(a, b, preferred_element_type=F32)


def flip(x):
    n = x.shape[1]
    eye = (
        lax.broadcasted_iota(jnp.int32, (n, n), 0) == lax.broadcasted_iota(jnp.int32, (n, n), 1)
    ).astype(BF16)
    return lax.dot_general(
        eye, x, (((1,), (1,)), ((), ())), preferred_element_type=F32
    ).astype(BF16)


def regroup(x, outer, inner):
    n = outer * inner
    row = lax.broadcasted_iota(jnp.int32, (n, n), 0)
    col = lax.broadcasted_iota(jnp.int32, (n, n), 1)
    place = (col == (row % outer) * inner + row // outer).astype(BF16)
    return dot(place, x).astype(BF16)


def mixer_kernel(
    sizes,
    ig_hbm, va_hbm, og_hbm, go_hbm, gain_hbm, taps_hbm, entry_nat_hbm, cos_hbm, sin_hbm, fwd_hbm,
    entry_hbm, inv_hbm, leave_hbm, leave_nat_hbm,
    gin, gval, gout, filter_out, skip_out,
    ig, va, og, go, gain, taps, entry_nat_in, cos, sin, fwd_in, entry_in, inv_in, leave_in,
    leave_nat_in, taps_rows, entry_nat, fwd, entry, inv, leave, leave_nat,
    send1, recv1, send2, recv2, send3, recv3, send4, recv4,
    near_sum, near_recv, far_sum, far_recv, fsend, frecv, dp_sum, dp_recv, word, words, kern,
    load_sem, send_sem, recv_sem, fsend_sem, frecv_sem, dsend_sem, drecv_sem,
    wsend_sem, wrecv_sem,
):
    n_dp, far, near, chans, block = sizes
    ctx = far * near
    outer = 2 * ctx
    d = lax.axis_index("dp")
    c = lax.axis_index("context")
    g = c // near
    h = c % near

    pairs = (
        (ig_hbm, ig), (va_hbm, va), (og_hbm, og), (go_hbm, go), (taps_hbm, taps),
        (entry_nat_hbm, entry_nat_in), (cos_hbm, cos), (sin_hbm, sin), (fwd_hbm, fwd_in),
        (entry_hbm, entry_in), (inv_hbm, inv_in), (leave_hbm, leave_in),
        (leave_nat_hbm, leave_nat_in), (gain_hbm, gain),
    )
    loads = [pltpu.make_async_copy(src, dst, load_sem.at[i]) for i, (src, dst) in enumerate(pairs)]
    for load in loads[:4]:
        load.start()

    def far_peer(i):
        t = lax.rem(g + i, far)
        return t, (d, t * near + h)

    def near_peer(i):
        t = lax.rem(h + i, near)
        return t, (d, g * near + t)

    barrier = pltpu.get_barrier_semaphore()

    def greet(peer):
        def step(i, carry):
            pl.semaphore_signal(barrier, inc=1, device_id=peer(i)[1], device_id_type=MESH)
            return carry

        return step

    half = n_dp // 2

    def order(t):
        return t + (t // half) * (half - 1 - 2 * lax.rem(t, half))

    ahead = order(d)
    others = [lax.rem(d + n_dp - i, n_dp) for i in (2, 1, 3)[: n_dp - 1]] if n_dp > 2 else [1 - d]
    lax.fori_loop(1, far, greet(far_peer), 0)
    lax.fori_loop(1, near, greet(near_peer), 0)
    for t in others:

        @pl.when(order(t) > ahead)
        def _():
            pl.semaphore_signal(barrier, inc=1, device_id=(t, c), device_id_type=MESH)

    for load in loads[4:]:
        load.start()

    def send_all(peer, count, src, dst, own, sem):
        def step(i, carry):
            t, target = peer(i)
            pltpu.make_async_remote_copy(
                src_ref=src(t),
                dst_ref=dst.at[own],
                send_sem=send_sem.at[sem],
                recv_sem=recv_sem.at[sem],
                device_id=target,
                device_id_type=MESH,
            ).start()
            return carry

        lax.fori_loop(1, count, step, 0)

    def wait_blocks(dst, count, sems, i):
        part = dst.at[pl.ds(0, count - 1)]
        pltpu.make_async_copy(part, part, sems.at[i]).wait()

    def wait_one(ref, sem):
        pltpu.make_async_copy(ref, ref, sem).wait()

    def total(blocks, count):
        value = blocks[0]
        for i in range(1, count):
            value = value + blocks[i]
        return value

    def product(a, b):
        return (a[...].astype(F32) * b[...].astype(F32)).astype(BF16)

    for i in range(4):
        loads[i].wait()
    mixed, gmix = product(ig, va), product(go, og)
    for i, tokens in enumerate((mixed, gmix)):
        send1[i] = flip(tokens).reshape(far, 2 * near, block)
        recv1[i, g] = send1[i, g]
    near_sum[...] = jnp.sum(mixed.astype(F32) * gmix.astype(F32), axis=0, keepdims=True)
    near_recv[h] = near_sum[...]
    word[...] = jnp.zeros(word.shape, F32)

    pl.semaphore_wait(barrier, far + near - 2 + ahead)
    for i in range(2):
        send_all(far_peer, far, lambda t: send1.at[i, t], recv1.at[i], g, i)
    send_all(near_peer, near, lambda t: near_sum, near_recv, h, 8)
    for t in others:

        @pl.when(order(t) < ahead)
        def _():
            pltpu.make_async_remote_copy(
                src_ref=word,
                dst_ref=words.at[d],
                send_sem=wsend_sem.at[t],
                recv_sem=wrecv_sem.at[d],
                device_id=(t, c),
                device_id_type=MESH,
            ).start()

    def forward(table, x):
        section = dot(table, x)
        out = []
        for i in range(x.shape[1] // block):
            re = section[:outer, i * block : (i + 1) * block]
            im = section[outer:, i * block : (i + 1) * block]
            turned = jnp.concatenate(
                [
                    (re * cos[...] + im * sin[...]).astype(BF16),
                    (im * cos[...] - re * sin[...]).astype(BF16),
                ],
                1,
            )
            out.append(dot(turned, fwd[...]))
        return out

    def inverse(table, spectra):
        real, imag = [], []
        for spectrum in spectra:
            back = dot(spectrum, inv[...])
            re, im = back[:, :block], back[:, block:]
            real.append((re * cos[...] - im * sin[...]).astype(BF16))
            imag.append((im * cos[...] + re * sin[...]).astype(BF16))
        turned = jnp.concatenate([jnp.concatenate(real, 1), jnp.concatenate(imag, 1)], 0)
        return dot(table, turned).astype(BF16)

    for i in range(4, 14):
        loads[i].wait()
    entry_nat[...] = entry_nat_in[...].astype(BF16)
    fwd[...] = fwd_in[...].astype(BF16)
    for j in range(2):
        for a in range(ctx):
            taps_rows[j, pl.ds(a, 1)] = taps[pl.ds(j, 1), pl.ds(a * block, block)].astype(F32)
    both = jnp.concatenate([taps_rows[0], taps_rows[1]], 1).astype(BF16)
    for j, spectrum in enumerate(forward(entry_nat[...], both)):
        kern[j] = spectrum
    entry[...] = entry_in[...].astype(BF16)
    inv[...] = inv_in[...].astype(BF16)
    leave[...] = leave_in[...].astype(BF16)
    leave_nat[...] = leave_nat_in[...].astype(BF16)

    for i in range(2):
        wait_blocks(recv1.at[i], far, recv_sem, i)
        rows = regroup(recv1[i].reshape(chans, block), far, 2 * near)
        send2[i] = rows.reshape(near, 2, far, block)
        recv2[i, h] = send2[i, h]
        send_all(near_peer, near, lambda t: send2.at[i, t], recv2.at[i], h, 2 + i)

    wait_blocks(near_recv, near, recv_sem, 8)
    far_sum[...] = total(near_recv, near)
    far_recv[g] = far_sum[...]
    send_all(far_peer, far, lambda t: far_sum, far_recv, g, 9)

    spectra = []
    for i in range(2):
        wait_blocks(recv2.at[i], near, recv_sem, 2 + i)
        both = jnp.concatenate([recv2[i, :, j].reshape(ctx, block) for j in range(2)], 1)
        spectra.append([(s[:, :block], s[:, block:]) for s in forward(entry[...], both)])
    sources, gradients = spectra

    specs = []
    for (ur, ui), (vr, vi) in zip(sources, gradients):
        specs.append(jnp.concatenate([ur * vr + ui * vi, ur * vi - ui * vr], 1).astype(BF16))
    term = inverse(leave_nat[...], specs)
    for j in range(2):
        part = term[:, j * block : (j + 1) * block]
        fsend[:, j] = part.reshape(n_dp, ctx // n_dp, block)
    frecv[d] = fsend[d]
    wait_blocks(far_recv, far, recv_sem, 9)
    dp_sum[...] = total(far_recv, far)
    dp_recv[d] = dp_sum[...]

    def send_shares(t):
        for src, dst, out, come in (
            (fsend.at[t], frecv.at[d], fsend_sem.at[t], frecv_sem.at[d]),
            (dp_sum, dp_recv.at[d], dsend_sem.at[t], drecv_sem.at[d]),
        ):
            pltpu.make_async_remote_copy(
                src_ref=src,
                dst_ref=dst,
                send_sem=out,
                recv_sem=come,
                device_id=(t, c),
                device_id_type=MESH,
            ).start()

    for t in others:

        @pl.when(order(t) < ahead)
        def _():
            send_shares(t)

    kernels = [(kern[j][:, :block], kern[j][:, block:]) for j in range(2)]
    convs, backs = [], []
    for (ur, ui), (vr, vi), (kr, ki) in zip(sources, gradients, kernels):
        convs.append(jnp.concatenate([ur * kr - ui * ki, ur * ki + ui * kr], 1).astype(BF16))
        backs.append(jnp.concatenate([kr * vr + ki * vi, kr * vi - ki * vr], 1).astype(BF16))
    for i, specs in enumerate((convs, backs)):
        both = inverse(leave[...], specs)
        for j in range(2):
            part = both[:, j * block : (j + 1) * block]
            send3[i, :, j] = part.reshape(near, far, block)
        recv3[i, h] = send3[i, h]
        send_all(near_peer, near, lambda t: send3.at[i, t], recv3.at[i], h, 4 + i)

    for t in others:

        @pl.when(order(t) > ahead)
        def _():
            wait_one(words.at[t], wrecv_sem.at[t])
            send_shares(t)

    for i in range(2):
        wait_blocks(recv3.at[i], near, recv_sem, 4 + i)
        rows = regroup(recv3[i].reshape(chans, block), 2 * near, far)
        send4[i] = rows.reshape(far, 2 * near, block)
        recv4[i, g] = send4[i, g]
        send_all(far_peer, far, lambda t: send4.at[i, t], recv4.at[i], g, 6 + i)

    wait_blocks(recv4.at[0], far, recv_sem, 6)
    conv = flip(recv4[0].reshape(chans, block)).astype(F32)
    gains = gain[...]
    gout[...] = (
        go[...].astype(F32) * (conv + gains * product(ig, va).astype(F32))
    ).astype(BF16)
    wait_blocks(recv4.at[1], far, recv_sem, 7)
    back = flip(recv4[1].reshape(chans, block)).astype(F32)
    grad_mixed = back + gains * product(go, og).astype(F32)
    gin[...] = (grad_mixed * va[...].astype(F32)).astype(BF16)
    gval[...] = (grad_mixed * ig[...].astype(F32)).astype(BF16)

    for t in others:
        wait_one(frecv.at[t], frecv_sem.at[t])
    scale = 1.0 / math.sqrt(n_dp * ctx * block)
    grad = frecv[0].astype(F32)
    for i in range(1, n_dp):
        grad = grad + frecv[i].astype(F32)
    grad = grad * scale
    for j in range(2):
        for a in range(ctx // n_dp):
            filter_out[pl.ds(j, 1), pl.ds(a * block, block)] = grad[j, a : a + 1]
    for t in others:
        wait_one(dp_recv.at[t], drecv_sem.at[t])
    skip_out[...] = total(dp_recv, n_dp) * scale

    for i in range(2):
        wait_blocks(recv1.at[i], far, send_sem, i)
        wait_blocks(recv2.at[i], near, send_sem, 2 + i)
        wait_blocks(recv3.at[i], near, send_sem, 4 + i)
        wait_blocks(recv4.at[i], far, send_sem, 6 + i)
    wait_blocks(near_recv, near, send_sem, 8)
    wait_blocks(far_recv, far, send_sem, 9)
    for t in others:
        wait_one(fsend.at[t], fsend_sem.at[t])
        wait_one(dp_sum, dsend_sem.at[t])

        @pl.when(order(t) < ahead)
        def _():
            wait_one(word, wsend_sem.at[t])


def copy_kernel(*refs):
    n = (len(refs) - 1) // 2
    copies = [pltpu.make_async_copy(refs[i], refs[n + i], refs[-1].at[i]) for i in range(n)]
    for copy in copies:
        copy.start()
    for copy in copies:
        copy.wait()


def per_device(input_gate, values, output_gate, grad_out, filter_taps, skip_gain):
    n_dp = lax.axis_size("dp")
    ctx = lax.axis_size("context")
    far, near = group_sizes(ctx)
    block, chans = input_gate.shape[1:]
    rows = np.arange(ctx).reshape(far, near).T.reshape(-1)
    tables = dft_tables(ctx, block, rows, 1.0 / (2 * ctx * block))
    gates = (input_gate[0], values[0], output_gate[0], grad_out[0], skip_gain.reshape(1, -1))
    operands = gates + (filter_taps,) + tables
    share = ctx // n_dp
    outs = tuple(jax.ShapeDtypeStruct((block, chans), BF16) for _ in range(3)) + (
        jax.ShapeDtypeStruct((2, share * block), F32),
        jax.ShapeDtypeStruct((1, chans), F32),
    )
    vmem = pltpu.VMEM
    dma = pltpu.SemaphoreType.DMA
    results = pl.pallas_call(
        functools.partial(mixer_kernel, (n_dp, far, near, chans, block)),
        out_shape=tuple(pltpu.VMEM(x.shape, x.dtype) for x in outs),
        in_specs=[pl.BlockSpec(memory_space=pltpu.HBM)] * len(operands),
        out_specs=tuple(pl.BlockSpec(memory_space=pltpu.VMEM) for _ in outs),
        scratch_shapes=[vmem(x.shape, x.dtype) for x in operands]
        + [vmem((2, ctx, block), F32)]
        + [vmem(tables[i].shape, BF16) for i in (0, 3, 4, 5, 6, 7)]
        + [vmem((2, far, 2 * near, block), BF16)] * 2
        + [vmem((2, near, 2, far, block), BF16)] * 4
        + [vmem((2, far, 2 * near, block), BF16)] * 2
        + [vmem((1, chans), F32), vmem((near, 1, chans), F32)]
        + [vmem((1, chans), F32), vmem((far, 1, chans), F32)]
        + [vmem((n_dp, 2, share, block), BF16)] * 2
        + [vmem((1, chans), F32), vmem((n_dp, 1, chans), F32)]
        + [vmem((1, 128), F32), vmem((n_dp, 1, 128), F32)]
        + [vmem((2, 2 * ctx, 2 * block), F32)]
        + [dma((len(operands),)), dma((10,)), dma((10,))]
        + [dma((n_dp,))] * 6,
        compiler_params=pltpu.CompilerParams(
            collective_id=0, has_side_effects=True, vmem_limit_bytes=32 * 1024 * 1024
        ),
        name="mixer",
    )(*(pltpu.with_memory_space_constraint(x, pltpu.HBM) for x in operands))
    grad_input, grad_value, grad_output, filter_grad, skip_grad = pl.pallas_call(
        copy_kernel,
        out_shape=outs,
        in_specs=[pl.BlockSpec(memory_space=pltpu.VMEM)] * len(outs),
        out_specs=tuple(pl.BlockSpec(memory_space=pl.ANY) for _ in outs),
        scratch_shapes=[dma((len(outs),))],
        compiler_params=pltpu.CompilerParams(vmem_limit_bytes=32 * 1024 * 1024),
        name="results",
    )(*results)
    return (
        grad_input[None],
        grad_value[None],
        grad_output[None],
        filter_grad,
        skip_grad.reshape(-1),
    )


def solution(mesh):
    return jax.shard_map(
        per_device,
        mesh=mesh,
        in_specs=(
            P("dp", "context", None),
            P("dp", "context", None),
            P("dp", "context", None),
            P("dp", "context", None),
            P("context", None),
            P(),
        ),
        out_specs=(
            P("dp", "context", None),
            P("dp", "context", None),
            P("dp", "context", None),
            P("context", "dp"),
            P(),
        ),
        check_vma=False,
    )
```

```python
import functools
import math

import jax
import jax.numpy as jnp
import numpy as np
from jax import lax
from jax.experimental import pallas as pl
from jax.experimental.pallas import tpu as pltpu
from jax.sharding import PartitionSpec as P

MESH = pl.DeviceIdType.MESH
F32 = jnp.float32
BF16 = jnp.bfloat16


def group_sizes(context):
    near = 1
    while 2 * near * near * 2 <= context:
        near *= 2
    return context // near, near


def dft_tables(pieces, block_len, scale):
    outer = 2 * pieces
    total = outer * block_len

    def angle(first, second, modulus):
        return (first[:, None] * second[None, :] % modulus) * (2.0 * math.pi / modulus)

    across = np.arange(pieces)
    outer_index = np.arange(outer)
    inner_index = np.arange(block_len)
    first = angle(outer_index, across, outer)
    entry = np.concatenate([np.cos(first), -np.sin(first)], 0)
    twist = angle(outer_index, inner_index, total)
    twist_cos, twist_sin = np.cos(twist), np.sin(twist)
    inner = angle(inner_index, inner_index, block_len)
    cosine, sine = np.cos(inner), np.sin(inner)
    forward_inner = np.block([[cosine, -sine], [sine, cosine]])
    inverse_inner = np.block([[cosine, sine], [-sine, cosine]])
    last = angle(across, outer_index, outer)
    leave = np.concatenate([np.cos(last), -np.sin(last)], 1) * scale

    def low(table):
        return table.astype(BF16).astype(np.float32)

    return (
        low(entry),
        twist_cos.astype(np.float32),
        twist_sin.astype(np.float32),
        low(forward_inner),
        low(inverse_inner),
        low(leave),
    )


def dot(a, b):
    return jnp.dot(a, b, preferred_element_type=F32)


def dot_rows(a, b):
    return lax.dot_general(a, b, (((1,), (1,)), ((), ())), preferred_element_type=F32)


def selector(n, place):
    row = lax.broadcasted_iota(jnp.int32, (n, n), 0)
    col = lax.broadcasted_iota(jnp.int32, (n, n), 1)
    return (col == place(row)).astype(BF16)


def mixer_kernel(
    sizes,
    ig_hbm, va_hbm, og_hbm, go_hbm, gain_hbm, taps_hbm, entry_hbm, cos_hbm, sin_hbm, fwd_hbm,
    inv_hbm, leave_hbm,
    gin, gval, gout, filter_out, skip_out,
    ig, va, og, go, gain, taps, entry_in, cos, sin, fwd_in, inv_in, leave_in,
    taps_rows, entry, fwd, inv, leave, by_channel, by_piece, of_piece,
    there_out, there_in, back_out, back_in,
    near_sum, near_recv, far_sum, far_recv, fsend, frecv, dp_sum, dp_recv, word, words, kern,
    load_sem, send_sem, recv_sem, fsend_sem, frecv_sem, dsend_sem, drecv_sem,
    wsend_sem, wrecv_sem, ready,
):
    n_dp, far, near, chans, block = sizes
    ctx = far * near
    outer = 2 * ctx
    d = lax.axis_index("dp")
    c = lax.axis_index("context")
    g = c // near
    h = c % near

    pairs = (
        (ig_hbm, ig), (va_hbm, va), (og_hbm, og), (go_hbm, go), (taps_hbm, taps),
        (entry_hbm, entry_in), (cos_hbm, cos), (sin_hbm, sin), (fwd_hbm, fwd_in),
        (inv_hbm, inv_in), (leave_hbm, leave_in), (gain_hbm, gain),
    )
    loads = [pltpu.make_async_copy(src, dst, load_sem.at[i]) for i, (src, dst) in enumerate(pairs)]
    for load in loads[:4]:
        load.start()

    def far_peer(i):
        t = lax.rem(g + i, far)
        return t, (d, t * near + h)

    def near_peer(i):
        t = lax.rem(h + i, near)
        return t, (d, g * near + t)

    def any_peer(i):
        t = lax.rem(c + i, ctx)
        return t, (d, t)

    barrier = pltpu.get_barrier_semaphore()

    def greet(peer):
        def step(i, carry):
            pl.semaphore_signal(barrier, inc=1, device_id=peer(i)[1], device_id_type=MESH)
            return carry

        return step

    half = n_dp // 2

    def order(t):
        return t + (t // half) * (half - 1 - 2 * lax.rem(t, half))

    ahead = order(d)
    others = [lax.rem(d + n_dp - i, n_dp) for i in (2, 1, 3)[: n_dp - 1]] if n_dp > 2 else [1 - d]
    lax.fori_loop(1, far, greet(far_peer), 0)
    lax.fori_loop(1, near, greet(near_peer), 0)
    for t in others:

        @pl.when(order(t) > ahead)
        def _():
            pl.semaphore_signal(barrier, inc=1, device_id=(t, c), device_id_type=MESH)

    for load in loads[4:]:
        load.start()

    part = ctx // 2
    by_channel[...] = selector(
        4 * part, lambda r: (r % 4) // 2 * ctx + r // 4 * 2 + r % 2
    )
    by_piece[...] = selector(4 * part, lambda r: r % 4 * part + r // 4)
    of_piece[...] = selector(4 * part, lambda r: r % part * 4 + r // part)

    def send_all(peer, count, src, dst, own, sem):
        def step(i, carry):
            t, target = peer(i)
            pltpu.make_async_remote_copy(
                src_ref=src(t),
                dst_ref=dst.at[own],
                send_sem=send_sem.at[sem],
                recv_sem=recv_sem.at[sem],
                device_id=target,
                device_id_type=MESH,
            ).start()
            return carry

        lax.fori_loop(1, count, step, 0)

    def wait_blocks(dst, count, sems, i):
        blocks = dst.at[pl.ds(0, count - 1)]
        pltpu.make_async_copy(blocks, blocks, sems.at[i]).wait()

    def wait_one(ref, sem):
        pltpu.make_async_copy(ref, ref, sem).wait()

    def total(blocks, count):
        value = blocks[0]
        for i in range(1, count):
            value = value + blocks[i]
        return value

    def product(a, b):
        return (a[...].astype(F32) * b[...].astype(F32)).astype(BF16)

    for i in range(4):
        loads[i].wait()
    mixed, gmix = product(ig, va), product(go, og)
    for q in range(2):
        lanes = slice(q * ctx, (q + 1) * ctx)
        rows = dot_rows(by_channel[...], jnp.concatenate([mixed[:, lanes], gmix[:, lanes]], 1))
        there_out[pl.ds(q * part, part)] = rows.astype(BF16).reshape(part, 4, block)
    there_in[c] = there_out[c]
    near_sum[...] = jnp.sum(mixed.astype(F32) * gmix.astype(F32), axis=0, keepdims=True)
    near_recv[h] = near_sum[...]
    word[...] = jnp.zeros(word.shape, F32)

    pl.semaphore_wait(barrier, far + near - 2 + ahead)

    def second(i, carry):
        pl.semaphore_signal(ready, inc=1, device_id=near_peer(i)[1], device_id_type=MESH)
        return carry

    lax.fori_loop(1, near, second, 0)

    def send_there(i, k):
        t = lax.rem(g + i, far) * near + lax.rem(h + k, near)
        pltpu.make_async_remote_copy(
            src_ref=there_out.at[t],
            dst_ref=there_in.at[c],
            send_sem=send_sem.at[0],
            recv_sem=recv_sem.at[0],
            device_id=(d, t),
            device_id_type=MESH,
        ).start()

    def far_step(i, carry):
        send_there(i, 0)
        return carry

    def near_step(k, carry):
        send_there(0, k)
        return carry

    def other_step(k, carry):
        def step(i, inner):
            send_there(i, k)
            return inner

        return lax.fori_loop(1, far, step, carry)

    lax.fori_loop(1, far, far_step, 0)
    lax.fori_loop(1, near, near_step, 0)
    pl.semaphore_wait(ready, near - 1)
    lax.fori_loop(1, near, other_step, 0)
    send_all(near_peer, near, lambda t: near_sum, near_recv, h, 2)
    for t in others:

        @pl.when(order(t) < ahead)
        def _():
            pltpu.make_async_remote_copy(
                src_ref=word,
                dst_ref=words.at[d],
                send_sem=wsend_sem.at[t],
                recv_sem=wrecv_sem.at[d],
                device_id=(t, c),
                device_id_type=MESH,
            ).start()

    def forward(table, x):
        section = dot(table, x)
        out = []
        for i in range(x.shape[1] // block):
            re = section[:outer, i * block : (i + 1) * block]
            im = section[outer:, i * block : (i + 1) * block]
            turned = jnp.concatenate(
                [
                    (re * cos[...] + im * sin[...]).astype(BF16),
                    (im * cos[...] - re * sin[...]).astype(BF16),
                ],
                1,
            )
            out.append(dot(turned, fwd[...]))
        return out

    def inverse(table, spectra):
        real, imag = [], []
        for spectrum in spectra:
            back = dot(spectrum, inv[...])
            re, im = back[:, :block], back[:, block:]
            real.append((re * cos[...] - im * sin[...]).astype(BF16))
            imag.append((im * cos[...] + re * sin[...]).astype(BF16))
        turned = jnp.concatenate([jnp.concatenate(real, 1), jnp.concatenate(imag, 1)], 0)
        return dot(table, turned).astype(BF16)

    for i in range(4, 12):
        loads[i].wait()
    entry[...] = entry_in[...].astype(BF16)
    fwd[...] = fwd_in[...].astype(BF16)
    for j in range(2):
        for a in range(ctx):
            taps_rows[j, pl.ds(a, 1)] = taps[pl.ds(j, 1), pl.ds(a * block, block)].astype(F32)
    both = jnp.concatenate([taps_rows[0], taps_rows[1]], 1).astype(BF16)
    for j, spectrum in enumerate(forward(entry[...], both)):
        kern[j] = spectrum
    inv[...] = inv_in[...].astype(BF16)
    leave[...] = leave_in[...].astype(BF16)

    wait_blocks(near_recv, near, recv_sem, 2)
    far_sum[...] = total(near_recv, near)
    far_recv[g] = far_sum[...]
    send_all(far_peer, far, lambda t: far_sum, far_recv, g, 3)

    wait_blocks(there_in, ctx, recv_sem, 0)
    halves = []
    for q in range(2):
        rows = there_in[pl.ds(q * part, part)].reshape(4 * part, block)
        halves.append(dot(of_piece[...], rows).astype(BF16))
    lines = [
        jnp.concatenate([rows[i * part : (i + 1) * part] for rows in halves], 0) for i in range(4)
    ]
    spectra = []
    for i in range(2):
        both = jnp.concatenate(lines[2 * i : 2 * i + 2], 1)
        spectra.append([(s[:, :block], s[:, block:]) for s in forward(entry[...], both)])
    sources, gradients = spectra

    specs = []
    for (ur, ui), (vr, vi) in zip(sources, gradients):
        specs.append(jnp.concatenate([ur * vr + ui * vi, ur * vi - ui * vr], 1).astype(BF16))
    term = inverse(leave[...], specs)
    for j in range(2):
        line = term[:, j * block : (j + 1) * block]
        fsend[:, j] = line.reshape(n_dp, ctx // n_dp, block)
    frecv[d] = fsend[d]
    wait_blocks(far_recv, far, recv_sem, 3)
    dp_sum[...] = total(far_recv, far)
    dp_recv[d] = dp_sum[...]

    def send_shares(t):
        for src, dst, out, come in (
            (fsend.at[t], frecv.at[d], fsend_sem.at[t], frecv_sem.at[d]),
            (dp_sum, dp_recv.at[d], dsend_sem.at[t], drecv_sem.at[d]),
        ):
            pltpu.make_async_remote_copy(
                src_ref=src,
                dst_ref=dst,
                send_sem=out,
                recv_sem=come,
                device_id=(t, c),
                device_id_type=MESH,
            ).start()

    for t in others:

        @pl.when(order(t) < ahead)
        def _():
            send_shares(t)

    kernels = [(kern[j][:, :block], kern[j][:, block:]) for j in range(2)]
    convs, backs = [], []
    for (ur, ui), (vr, vi), (kr, ki) in zip(sources, gradients, kernels):
        convs.append(jnp.concatenate([ur * kr - ui * ki, ur * ki + ui * kr], 1).astype(BF16))
        backs.append(jnp.concatenate([kr * vr + ki * vi, kr * vi - ki * vr], 1).astype(BF16))
    lines = []
    for specs in (convs, backs):
        both = inverse(leave[...], specs)
        lines += [both[:, :block], both[:, block:]]
    for q in range(2):
        rows = jnp.concatenate([x[q * part : (q + 1) * part] for x in lines], 0)
        rows = dot(by_piece[...], rows).astype(BF16)
        back_out[pl.ds(q * part, part)] = rows.reshape(part, 4, block)
    back_in[c] = back_out[c]
    send_all(any_peer, ctx, lambda t: back_out.at[t], back_in, c, 1)

    for t in others:

        @pl.when(order(t) > ahead)
        def _():
            wait_one(words.at[t], wrecv_sem.at[t])
            send_shares(t)

    wait_blocks(back_in, ctx, recv_sem, 1)
    eye = selector(block, lambda r: r)
    convs, backs = [], []
    for q in range(2):
        rows = back_in[pl.ds(q * part, part)].reshape(4 * part, block)
        rows = dot(dot_rows(eye, rows).astype(BF16), by_channel[...])
        convs.append(rows[:, :ctx])
        backs.append(rows[:, ctx:])
    gains = gain[...]
    gout[...] = (
        go[...].astype(F32)
        * (jnp.concatenate(convs, 1) + gains * product(ig, va).astype(F32))
    ).astype(BF16)
    grad_mixed = jnp.concatenate(backs, 1) + gains * product(go, og).astype(F32)
    gin[...] = (grad_mixed * va[...].astype(F32)).astype(BF16)
    gval[...] = (grad_mixed * ig[...].astype(F32)).astype(BF16)

    for t in others:
        wait_one(frecv.at[t], frecv_sem.at[t])
    scale = 1.0 / math.sqrt(n_dp * ctx * block)
    grad = frecv[0].astype(F32)
    for i in range(1, n_dp):
        grad = grad + frecv[i].astype(F32)
    grad = grad * scale
    for j in range(2):
        for a in range(ctx // n_dp):
            filter_out[pl.ds(j, 1), pl.ds(a * block, block)] = grad[j, a : a + 1]
    for t in others:
        wait_one(dp_recv.at[t], drecv_sem.at[t])
    skip_out[...] = total(dp_recv, n_dp) * scale

    wait_blocks(there_in, ctx, send_sem, 0)
    wait_blocks(back_in, ctx, send_sem, 1)
    wait_blocks(near_recv, near, send_sem, 2)
    wait_blocks(far_recv, far, send_sem, 3)
    for t in others:
        wait_one(fsend.at[t], fsend_sem.at[t])
        wait_one(dp_sum, dsend_sem.at[t])

        @pl.when(order(t) < ahead)
        def _():
            wait_one(word, wsend_sem.at[t])


def copy_kernel(*refs):
    n = (len(refs) - 1) // 2
    copies = [pltpu.make_async_copy(refs[i], refs[n + i], refs[-1].at[i]) for i in range(n)]
    for copy in copies:
        copy.start()
    for copy in copies:
        copy.wait()


def per_device(input_gate, values, output_gate, grad_out, filter_taps, skip_gain):
    n_dp = lax.axis_size("dp")
    ctx = lax.axis_size("context")
    far, near = group_sizes(ctx)
    block, chans = input_gate.shape[1:]
    tables = dft_tables(ctx, block, 1.0 / (2 * ctx * block))
    gates = (input_gate[0], values[0], output_gate[0], grad_out[0], skip_gain.reshape(1, -1))
    operands = gates + (filter_taps,) + tables
    share = ctx // n_dp
    outs = tuple(jax.ShapeDtypeStruct((block, chans), BF16) for _ in range(3)) + (
        jax.ShapeDtypeStruct((2, share * block), F32),
        jax.ShapeDtypeStruct((1, chans), F32),
    )
    vmem = pltpu.VMEM
    dma = pltpu.SemaphoreType.DMA
    results = pl.pallas_call(
        functools.partial(mixer_kernel, (n_dp, far, near, chans, block)),
        out_shape=tuple(pltpu.VMEM(x.shape, x.dtype) for x in outs),
        in_specs=[pl.BlockSpec(memory_space=pltpu.HBM)] * len(operands),
        out_specs=tuple(pl.BlockSpec(memory_space=pltpu.VMEM) for _ in outs),
        scratch_shapes=[vmem(x.shape, x.dtype) for x in operands]
        + [vmem((2, ctx, block), F32)]
        + [vmem(tables[i].shape, BF16) for i in (0, 3, 4, 5)]
        + [vmem((2 * ctx, 2 * ctx), BF16)] * 3
        + [vmem((ctx, 4, block), BF16)] * 4
        + [vmem((1, chans), F32), vmem((near, 1, chans), F32)]
        + [vmem((1, chans), F32), vmem((far, 1, chans), F32)]
        + [vmem((n_dp, 2, share, block), BF16)] * 2
        + [vmem((1, chans), F32), vmem((n_dp, 1, chans), F32)]
        + [vmem((1, 128), F32), vmem((n_dp, 1, 128), F32)]
        + [vmem((2, 2 * ctx, 2 * block), F32)]
        + [dma((len(operands),)), dma((4,)), dma((4,))]
        + [dma((n_dp,))] * 6
        + [pltpu.SemaphoreType.REGULAR],
        compiler_params=pltpu.CompilerParams(
            collective_id=0, has_side_effects=True, vmem_limit_bytes=32 * 1024 * 1024
        ),
        name="mixer",
    )(*(pltpu.with_memory_space_constraint(x, pltpu.HBM) for x in operands))
    grad_input, grad_value, grad_output, filter_grad, skip_grad = pl.pallas_call(
        copy_kernel,
        out_shape=outs,
        in_specs=[pl.BlockSpec(memory_space=pltpu.VMEM)] * len(outs),
        out_specs=tuple(pl.BlockSpec(memory_space=pl.ANY) for _ in outs),
        scratch_shapes=[dma((len(outs),))],
        compiler_params=pltpu.CompilerParams(vmem_limit_bytes=32 * 1024 * 1024),
        name="results",
    )(*results)
    return (
        grad_input[None],
        grad_value[None],
        grad_output[None],
        filter_grad,
        skip_grad.reshape(-1),
    )


def solution(mesh):
    return jax.shard_map(
        per_device,
        mesh=mesh,
        in_specs=(
            P("dp", "context", None),
            P("dp", "context", None),
            P("dp", "context", None),
            P("dp", "context", None),
            P("context", None),
            P(),
        ),
        out_specs=(
            P("dp", "context", None),
            P("dp", "context", None),
            P("dp", "context", None),
            P("context", "dp"),
            P(),
        ),
        check_vma=False,
    )
```

```python
import functools
import math

import jax
import jax.numpy as jnp
import numpy as np
from jax import lax
from jax.experimental import pallas as pl
from jax.experimental.pallas import tpu as pltpu
from jax.sharding import PartitionSpec as P

MESH = pl.DeviceIdType.MESH
F32 = jnp.float32
BF16 = jnp.bfloat16


def group_sizes(context):
    near = 1
    while 2 * near * near * 2 <= context:
        near *= 2
    return context // near, near


def dft_tables(pieces, block_len, scale):
    outer = 2 * pieces
    total = outer * block_len

    def angle(first, second, modulus):
        return (first[:, None] * second[None, :] % modulus) * (2.0 * math.pi / modulus)

    across = np.arange(pieces)
    outer_index = np.arange(outer)
    inner_index = np.arange(block_len)
    first = angle(outer_index, across, outer)
    entry = np.concatenate([np.cos(first), -np.sin(first)], 0)
    twist = angle(outer_index, inner_index, total)
    twist_cos, twist_sin = np.cos(twist), np.sin(twist)
    inner = angle(inner_index, inner_index, block_len)
    cosine, sine = np.cos(inner), np.sin(inner)
    forward_inner = np.block([[cosine, -sine], [sine, cosine]])
    inverse_inner = np.block([[cosine, sine], [-sine, cosine]])
    last = angle(across, outer_index, outer)
    leave = np.concatenate([np.cos(last), -np.sin(last)], 1) * scale

    def low(table):
        return table.astype(BF16).astype(np.float32)

    return (
        low(entry),
        twist_cos.astype(np.float32),
        twist_sin.astype(np.float32),
        low(forward_inner),
        low(inverse_inner),
        low(leave),
    )


def dot(a, b):
    return jnp.dot(a, b, preferred_element_type=F32)


def dot_rows(a, b):
    return lax.dot_general(a, b, (((1,), (1,)), ((), ())), preferred_element_type=F32)


def selector(n, place):
    row = lax.broadcasted_iota(jnp.int32, (n, n), 0)
    col = lax.broadcasted_iota(jnp.int32, (n, n), 1)
    return (col == place(row)).astype(BF16)


def mixer_kernel(
    sizes,
    ig_hbm, va_hbm, og_hbm, go_hbm, gain_hbm, taps_hbm, entry_hbm, cos_hbm, sin_hbm, fwd_hbm,
    inv_hbm, leave_hbm,
    gin, gval, gout, filter_out, skip_out,
    ig, va, og, go, gain, taps, entry_in, cos, sin, fwd_in, inv_in, leave_in,
    taps_rows, entry, fwd, inv, leave, by_channel, by_piece, of_piece,
    there_out, there_in, back_out, back_in,
    near_sum, near_recv, far_sum, far_recv, fsend, frecv, dp_sum, dp_recv, word, words, kern,
    load_sem, send_sem, recv_sem, fsend_sem, frecv_sem, dsend_sem, drecv_sem,
    wsend_sem, wrecv_sem, ready,
):
    n_dp, far, near, chans, block = sizes
    ctx = far * near
    outer = 2 * ctx
    d = lax.axis_index("dp")
    c = lax.axis_index("context")
    g = c // near
    h = c % near

    pairs = (
        (ig_hbm, ig), (va_hbm, va), (og_hbm, og), (go_hbm, go), (taps_hbm, taps),
        (entry_hbm, entry_in), (cos_hbm, cos), (sin_hbm, sin), (fwd_hbm, fwd_in),
        (inv_hbm, inv_in), (leave_hbm, leave_in), (gain_hbm, gain),
    )
    loads = [pltpu.make_async_copy(src, dst, load_sem.at[i]) for i, (src, dst) in enumerate(pairs)]

    def far_peer(i):
        t = lax.rem(g + i, far)
        return t, (d, t * near + h)

    def near_peer(i):
        t = lax.rem(h + i, near)
        return t, (d, g * near + t)

    n_y = int(math.isqrt(far))
    n_z, n_x = far // n_y, near // 2
    z, y, x, core = g // n_y, lax.rem(g, n_y), h // 2, lax.rem(h, 2)
    turns_y = sorted(range(n_y), key=lambda v: -min(v, n_y - v))
    turns_x = sorted(range(n_x), key=lambda v: -min(v, n_x - v))
    spots = [(i, j) for i in turns_x for j in (1, 0)]

    def around(act, spots):
        def step(s, carry):
            there = s + (1 - z // (n_z // 2)) * (n_z - 1 - 2 * s)
            for turn in turns_y:
                row = there * n_y + lax.rem(y + turn, n_y)

                def go():
                    for i, j in spots:
                        act(row * near + lax.rem(x + i, n_x) * 2 + lax.rem(core + j, 2))

                if turn == 0:
                    pl.when(row != g)(go)
                else:
                    go()
            return carry

        lax.fori_loop(0, n_z, step, 0)

    def within(act):
        for i, j in spots[:-1]:
            act(g * near + lax.rem(x + i, n_x) * 2 + lax.rem(core + j, 2))

    barrier = pltpu.get_barrier_semaphore()

    def greet(t):
        pl.semaphore_signal(barrier, inc=1, device_id=(d, t), device_id_type=MESH)

    half = n_dp // 2

    def order(t):
        return t + (t // half) * (half - 1 - 2 * lax.rem(t, half))

    ahead = order(d)
    others = [lax.rem(d + n_dp - i, n_dp) for i in (2, 1, 3)[: n_dp - 1]] if n_dp > 2 else [1 - d]
    around(greet, spots[-1:])
    within(greet)
    for t in others:

        @pl.when(order(t) > ahead)
        def _():
            pl.semaphore_signal(barrier, inc=1, device_id=(t, c), device_id_type=MESH)

    for load in loads:
        load.start()

    part = ctx // 2
    by_channel[...] = selector(
        4 * part, lambda r: (r % 4) // 2 * ctx + r // 4 * 2 + r % 2
    )
    by_piece[...] = selector(4 * part, lambda r: r % 4 * part + r // 4)
    of_piece[...] = selector(4 * part, lambda r: r % part * 4 + r // part)

    def send_all(peer, count, src, dst, own, sem):
        def step(i, carry):
            t, target = peer(i)
            pltpu.make_async_remote_copy(
                src_ref=src(t),
                dst_ref=dst.at[own],
                send_sem=send_sem.at[sem],
                recv_sem=recv_sem.at[sem],
                device_id=target,
                device_id_type=MESH,
            ).start()
            return carry

        lax.fori_loop(1, count, step, 0)

    def wait_blocks(dst, count, sems, i):
        blocks = dst.at[pl.ds(0, count - 1)]
        pltpu.make_async_copy(blocks, blocks, sems.at[i]).wait()

    def wait_one(ref, sem):
        pltpu.make_async_copy(ref, ref, sem).wait()

    def total(blocks, count):
        value = blocks[0]
        for i in range(1, count):
            value = value + blocks[i]
        return value

    def product(a, b):
        return (a[...].astype(F32) * b[...].astype(F32)).astype(BF16)

    for i in range(4):
        loads[i].wait()
    mixed, gmix = product(ig, va), product(go, og)
    for q in range(2):
        lanes = slice(q * ctx, (q + 1) * ctx)
        rows = dot_rows(by_channel[...], jnp.concatenate([mixed[:, lanes], gmix[:, lanes]], 1))
        there_out[pl.ds(q * part, part)] = rows.astype(BF16).reshape(part, 4, block)
    there_in[c] = there_out[c]
    near_sum[...] = jnp.sum(mixed.astype(F32) * gmix.astype(F32), axis=0, keepdims=True)
    near_recv[h] = near_sum[...]
    word[...] = jnp.zeros(word.shape, F32)

    pl.semaphore_wait(barrier, far + near - 2 + ahead)

    def second(t):
        pl.semaphore_signal(ready, inc=1, device_id=(d, t), device_id_type=MESH)

    within(second)

    def send_piece(src, dst, sem):
        def send(t):
            pltpu.make_async_remote_copy(
                src_ref=src.at[t],
                dst_ref=dst.at[c],
                send_sem=send_sem.at[sem],
                recv_sem=recv_sem.at[sem],
                device_id=(d, t),
                device_id_type=MESH,
            ).start()

        return send

    send_there = send_piece(there_out, there_in, 0)
    around(send_there, spots[-1:])
    send_all(near_peer, near, lambda t: near_sum, near_recv, h, 2)
    within(send_there)
    pl.semaphore_wait(ready, near - 1)
    around(send_there, spots[:-1])
    wait_blocks(near_recv, near, recv_sem, 2)
    far_sum[...] = total(near_recv, near)
    far_recv[g] = far_sum[...]
    send_all(far_peer, far, lambda t: far_sum, far_recv, g, 3)
    for t in others:

        @pl.when(order(t) < ahead)
        def _():
            pltpu.make_async_remote_copy(
                src_ref=word,
                dst_ref=words.at[d],
                send_sem=wsend_sem.at[t],
                recv_sem=wrecv_sem.at[d],
                device_id=(t, c),
                device_id_type=MESH,
            ).start()

    def forward(table, x):
        section = dot(table, x)
        out = []
        for i in range(x.shape[1] // block):
            re = section[:outer, i * block : (i + 1) * block]
            im = section[outer:, i * block : (i + 1) * block]
            turned = jnp.concatenate(
                [
                    (re * cos[...] + im * sin[...]).astype(BF16),
                    (im * cos[...] - re * sin[...]).astype(BF16),
                ],
                1,
            )
            out.append(dot(turned, fwd[...]))
        return out

    def inverse(table, spectra):
        real, imag = [], []
        for spectrum in spectra:
            back = dot(spectrum, inv[...])
            re, im = back[:, :block], back[:, block:]
            real.append((re * cos[...] - im * sin[...]).astype(BF16))
            imag.append((im * cos[...] + re * sin[...]).astype(BF16))
        turned = jnp.concatenate([jnp.concatenate(real, 1), jnp.concatenate(imag, 1)], 0)
        return dot(table, turned).astype(BF16)

    for i in range(4, 12):
        loads[i].wait()
    entry[...] = entry_in[...].astype(BF16)
    fwd[...] = fwd_in[...].astype(BF16)
    for j in range(2):
        for a in range(ctx):
            taps_rows[j, pl.ds(a, 1)] = taps[pl.ds(j, 1), pl.ds(a * block, block)].astype(F32)
    both = jnp.concatenate([taps_rows[0], taps_rows[1]], 1).astype(BF16)
    for j, spectrum in enumerate(forward(entry[...], both)):
        kern[j] = spectrum
    inv[...] = inv_in[...].astype(BF16)
    leave[...] = leave_in[...].astype(BF16)

    wait_blocks(there_in, ctx, recv_sem, 0)
    halves = []
    for q in range(2):
        rows = there_in[pl.ds(q * part, part)].reshape(4 * part, block)
        halves.append(dot(of_piece[...], rows).astype(BF16))
    lines = [
        jnp.concatenate([rows[i * part : (i + 1) * part] for rows in halves], 0) for i in range(4)
    ]
    spectra = []
    for i in range(2):
        both = jnp.concatenate(lines[2 * i : 2 * i + 2], 1)
        spectra.append([(s[:, :block], s[:, block:]) for s in forward(entry[...], both)])
    sources, gradients = spectra

    specs = []
    for (ur, ui), (vr, vi) in zip(sources, gradients):
        specs.append(jnp.concatenate([ur * vr + ui * vi, ur * vi - ui * vr], 1).astype(BF16))
    term = inverse(leave[...], specs)
    for j in range(2):
        line = term[:, j * block : (j + 1) * block]
        fsend[:, j] = line.reshape(n_dp, ctx // n_dp, block)
    frecv[d] = fsend[d]
    wait_blocks(far_recv, far, recv_sem, 3)
    dp_sum[...] = total(far_recv, far)
    dp_recv[d] = dp_sum[...]

    def send_shares(t):
        for src, dst, out, come in (
            (fsend.at[t], frecv.at[d], fsend_sem.at[t], frecv_sem.at[d]),
            (dp_sum, dp_recv.at[d], dsend_sem.at[t], drecv_sem.at[d]),
        ):
            pltpu.make_async_remote_copy(
                src_ref=src,
                dst_ref=dst,
                send_sem=out,
                recv_sem=come,
                device_id=(t, c),
                device_id_type=MESH,
            ).start()

    for t in others:

        @pl.when(order(t) < ahead)
        def _():
            send_shares(t)

    kernels = [(kern[j][:, :block], kern[j][:, block:]) for j in range(2)]
    convs, backs = [], []
    for (ur, ui), (vr, vi), (kr, ki) in zip(sources, gradients, kernels):
        convs.append(jnp.concatenate([ur * kr - ui * ki, ur * ki + ui * kr], 1).astype(BF16))
        backs.append(jnp.concatenate([kr * vr + ki * vi, kr * vi - ki * vr], 1).astype(BF16))
    lines = []
    for specs in (convs, backs):
        both = inverse(leave[...], specs)
        lines += [both[:, :block], both[:, block:]]
    for q in range(2):
        rows = jnp.concatenate([x[q * part : (q + 1) * part] for x in lines], 0)
        rows = dot(by_piece[...], rows).astype(BF16)
        back_out[pl.ds(q * part, part)] = rows.reshape(part, 4, block)
    back_in[c] = back_out[c]
    send_back = send_piece(back_out, back_in, 1)
    around(send_back, spots)
    within(send_back)

    for t in others:

        @pl.when(order(t) > ahead)
        def _():
            wait_one(words.at[t], wrecv_sem.at[t])
            send_shares(t)

    wait_blocks(back_in, ctx, recv_sem, 1)
    eye = selector(block, lambda r: r)
    convs, backs = [], []
    for q in range(2):
        rows = back_in[pl.ds(q * part, part)].reshape(4 * part, block)
        rows = dot(dot_rows(eye, rows).astype(BF16), by_channel[...])
        convs.append(rows[:, :ctx])
        backs.append(rows[:, ctx:])
    gains = gain[...]
    gout[...] = (
        go[...].astype(F32)
        * (jnp.concatenate(convs, 1) + gains * product(ig, va).astype(F32))
    ).astype(BF16)
    grad_mixed = jnp.concatenate(backs, 1) + gains * product(go, og).astype(F32)
    gin[...] = (grad_mixed * va[...].astype(F32)).astype(BF16)
    gval[...] = (grad_mixed * ig[...].astype(F32)).astype(BF16)

    for t in others:
        wait_one(frecv.at[t], frecv_sem.at[t])
    scale = 1.0 / math.sqrt(n_dp * ctx * block)
    grad = frecv[0].astype(F32)
    for i in range(1, n_dp):
        grad = grad + frecv[i].astype(F32)
    grad = grad * scale
    for j in range(2):
        for a in range(ctx // n_dp):
            filter_out[pl.ds(j, 1), pl.ds(a * block, block)] = grad[j, a : a + 1]
    for t in others:
        wait_one(dp_recv.at[t], drecv_sem.at[t])
    skip_out[...] = total(dp_recv, n_dp) * scale

    wait_blocks(there_in, ctx, send_sem, 0)
    wait_blocks(back_in, ctx, send_sem, 1)
    wait_blocks(near_recv, near, send_sem, 2)
    wait_blocks(far_recv, far, send_sem, 3)
    for t in others:
        wait_one(fsend.at[t], fsend_sem.at[t])
        wait_one(dp_sum, dsend_sem.at[t])

        @pl.when(order(t) < ahead)
        def _():
            wait_one(word, wsend_sem.at[t])


def copy_kernel(*refs):
    n = (len(refs) - 1) // 2
    copies = [pltpu.make_async_copy(refs[i], refs[n + i], refs[-1].at[i]) for i in range(n)]
    for copy in copies:
        copy.start()
    for copy in copies:
        copy.wait()


def per_device(input_gate, values, output_gate, grad_out, filter_taps, skip_gain):
    n_dp = lax.axis_size("dp")
    ctx = lax.axis_size("context")
    far, near = group_sizes(ctx)
    block, chans = input_gate.shape[1:]
    tables = dft_tables(ctx, block, 1.0 / (2 * ctx * block))
    gates = (input_gate[0], values[0], output_gate[0], grad_out[0], skip_gain.reshape(1, -1))
    operands = gates + (filter_taps,) + tables
    share = ctx // n_dp
    outs = tuple(jax.ShapeDtypeStruct((block, chans), BF16) for _ in range(3)) + (
        jax.ShapeDtypeStruct((2, share * block), F32),
        jax.ShapeDtypeStruct((1, chans), F32),
    )
    vmem = pltpu.VMEM
    dma = pltpu.SemaphoreType.DMA
    results = pl.pallas_call(
        functools.partial(mixer_kernel, (n_dp, far, near, chans, block)),
        out_shape=tuple(pltpu.VMEM(x.shape, x.dtype) for x in outs),
        in_specs=[pl.BlockSpec(memory_space=pltpu.HBM)] * len(operands),
        out_specs=tuple(pl.BlockSpec(memory_space=pltpu.VMEM) for _ in outs),
        scratch_shapes=[vmem(x.shape, x.dtype) for x in operands]
        + [vmem((2, ctx, block), F32)]
        + [vmem(tables[i].shape, BF16) for i in (0, 3, 4, 5)]
        + [vmem((2 * ctx, 2 * ctx), BF16)] * 3
        + [vmem((ctx, 4, block), BF16)] * 4
        + [vmem((1, chans), F32), vmem((near, 1, chans), F32)]
        + [vmem((1, chans), F32), vmem((far, 1, chans), F32)]
        + [vmem((n_dp, 2, share, block), BF16)] * 2
        + [vmem((1, chans), F32), vmem((n_dp, 1, chans), F32)]
        + [vmem((1, 128), F32), vmem((n_dp, 1, 128), F32)]
        + [vmem((2, 2 * ctx, 2 * block), F32)]
        + [dma((len(operands),)), dma((4,)), dma((4,))]
        + [dma((n_dp,))] * 6
        + [pltpu.SemaphoreType.REGULAR],
        compiler_params=pltpu.CompilerParams(
            collective_id=0, has_side_effects=True, vmem_limit_bytes=32 * 1024 * 1024
        ),
        name="mixer",
    )(*(pltpu.with_memory_space_constraint(x, pltpu.HBM) for x in operands))
    grad_input, grad_value, grad_output, filter_grad, skip_grad = pl.pallas_call(
        copy_kernel,
        out_shape=outs,
        in_specs=[pl.BlockSpec(memory_space=pltpu.VMEM)] * len(outs),
        out_specs=tuple(pl.BlockSpec(memory_space=pl.ANY) for _ in outs),
        scratch_shapes=[dma((len(outs),))],
        compiler_params=pltpu.CompilerParams(vmem_limit_bytes=32 * 1024 * 1024),
        name="results",
    )(*results)
    return (
        grad_input[None],
        grad_value[None],
        grad_output[None],
        filter_grad,
        skip_grad.reshape(-1),
    )


def solution(mesh):
    return jax.shard_map(
        per_device,
        mesh=mesh,
        in_specs=(
            P("dp", "context", None),
            P("dp", "context", None),
            P("dp", "context", None),
            P("dp", "context", None),
            P("context", None),
            P(),
        ),
        out_specs=(
            P("dp", "context", None),
            P("dp", "context", None),
            P("dp", "context", None),
            P("context", "dp"),
            P(),
        ),
        check_vma=False,
    )
```

```python
import functools
import math

import jax
import jax.numpy as jnp
import numpy as np
from jax import lax
from jax.experimental import pallas as pl
from jax.experimental.pallas import tpu as pltpu
from jax.sharding import PartitionSpec as P

MESH = pl.DeviceIdType.MESH
F32 = jnp.float32
BF16 = jnp.bfloat16


def group_sizes(context):
    near = 1
    while 2 * near * near * 2 <= context:
        near *= 2
    return context // near, near


def dft_tables(pieces, block_len, scale):
    outer = 2 * pieces
    total = outer * block_len

    def angle(first, second, modulus):
        return (first[:, None] * second[None, :] % modulus) * (2.0 * math.pi / modulus)

    across = np.arange(pieces)
    outer_index = np.arange(outer)
    inner_index = np.arange(block_len)
    first = angle(outer_index, across, outer)
    entry = np.concatenate([np.cos(first), -np.sin(first)], 0)
    twist = angle(outer_index, inner_index, total)
    twist_cos, twist_sin = np.cos(twist), np.sin(twist)
    inner = angle(inner_index, inner_index, block_len)
    cosine, sine = np.cos(inner), np.sin(inner)
    forward_inner = np.block([[cosine, -sine], [sine, cosine]])
    inverse_inner = np.block([[cosine, sine], [-sine, cosine]])
    last = angle(across, outer_index, outer)
    leave = np.concatenate([np.cos(last), -np.sin(last)], 1) * scale

    def low(table):
        return table.astype(BF16).astype(np.float32)

    return (
        low(entry),
        twist_cos.astype(np.float32),
        twist_sin.astype(np.float32),
        low(forward_inner),
        low(inverse_inner),
        low(leave),
    )


def dot(a, b):
    return jnp.dot(a, b, preferred_element_type=F32)


def dot_rows(a, b):
    return lax.dot_general(a, b, (((1,), (1,)), ((), ())), preferred_element_type=F32)


def selector(n, place):
    row = lax.broadcasted_iota(jnp.int32, (n, n), 0)
    col = lax.broadcasted_iota(jnp.int32, (n, n), 1)
    return (col == place(row)).astype(BF16)


def mixer_kernel(
    sizes,
    ig_hbm, va_hbm, og_hbm, go_hbm, gain_hbm, taps_hbm, entry_hbm, cos_hbm, sin_hbm, fwd_hbm,
    inv_hbm, leave_hbm,
    gin, gval, gout, filter_out, skip_out,
    ig, va, og, go, gain, taps, entry_in, cos, sin, fwd_in, inv_in, leave_in,
    taps_rows, entry, fwd, inv, leave, by_channel, by_piece, of_piece,
    there_out, there_in, back_out, back_in,
    near_sum, near_recv, far_sum, far_recv, fsend, frecv, dp_sum, dp_recv, word, words, kern,
    load_sem, send_sem, recv_sem, fsend_sem, frecv_sem, dsend_sem, drecv_sem,
    wsend_sem, wrecv_sem,
):
    n_dp, far, near, chans, block = sizes
    ctx = far * near
    outer = 2 * ctx
    d = lax.axis_index("dp")
    c = lax.axis_index("context")
    g = c // near
    h = c % near

    pairs = (
        (ig_hbm, ig), (va_hbm, va), (og_hbm, og), (go_hbm, go), (taps_hbm, taps),
        (entry_hbm, entry_in), (cos_hbm, cos), (sin_hbm, sin), (fwd_hbm, fwd_in),
        (inv_hbm, inv_in), (leave_hbm, leave_in), (gain_hbm, gain),
    )
    loads = [pltpu.make_async_copy(src, dst, load_sem.at[i]) for i, (src, dst) in enumerate(pairs)]

    def far_peer(i):
        t = lax.rem(g + i, far)
        return t, (d, t * near + h)

    def near_peer(i):
        t = lax.rem(h + i, near)
        return t, (d, g * near + t)

    n_y = int(math.isqrt(far))
    n_z, n_x = far // n_y, near // 2
    z, y, x, core = g // n_y, lax.rem(g, n_y), h // 2, lax.rem(h, 2)
    turns_y = sorted(range(n_y), key=lambda v: -min(v, n_y - v))
    turns_x = sorted(range(n_x), key=lambda v: -min(v, n_x - v))
    spots = [(i, j) for i in turns_x for j in (1, 0)]

    def around(act, spots):
        def step(s, carry):
            there = s + (1 - z // (n_z // 2)) * (n_z - 1 - 2 * s)
            for turn in turns_y:
                row = there * n_y + lax.rem(y + turn, n_y)

                def go():
                    for i, j in spots:
                        act(row * near + lax.rem(x + i, n_x) * 2 + lax.rem(core + j, 2))

                if turn == 0:
                    pl.when(row != g)(go)
                else:
                    go()
            return carry

        lax.fori_loop(0, n_z, step, 0)

    def within(act):
        for i, j in spots[:-1]:
            act(g * near + lax.rem(x + i, n_x) * 2 + lax.rem(core + j, 2))

    barrier = pltpu.get_barrier_semaphore()

    def greet(t):
        pl.semaphore_signal(barrier, inc=1, device_id=(d, t), device_id_type=MESH)

    half = n_dp // 2

    def order(t):
        return t + (t // half) * (half - 1 - 2 * lax.rem(t, half))

    ahead = order(d)
    others = [lax.rem(d + n_dp - i, n_dp) for i in (2, 1, 3)[: n_dp - 1]] if n_dp > 2 else [1 - d]
    for load in loads[:4]:
        load.start()
    around(greet, spots)
    within(greet)
    for t in others:

        @pl.when(order(t) > ahead)
        def _():
            pl.semaphore_signal(barrier, inc=1, device_id=(t, c), device_id_type=MESH)

    for load in loads[4:]:
        load.start()

    part = ctx // 2
    by_channel[...] = selector(
        4 * part, lambda r: (r % 4) // 2 * ctx + r // 4 * 2 + r % 2
    )
    by_piece[...] = selector(4 * part, lambda r: r % 4 * part + r // 4)
    of_piece[...] = selector(4 * part, lambda r: r % part * 4 + r // part)

    def send_all(peer, count, src, dst, own, sem):
        def step(i, carry):
            t, target = peer(i)
            pltpu.make_async_remote_copy(
                src_ref=src(t),
                dst_ref=dst.at[own],
                send_sem=send_sem.at[sem],
                recv_sem=recv_sem.at[sem],
                device_id=target,
                device_id_type=MESH,
            ).start()
            return carry

        lax.fori_loop(1, count, step, 0)

    def wait_blocks(dst, count, sems, i):
        blocks = dst.at[pl.ds(0, count - 1)]
        pltpu.make_async_copy(blocks, blocks, sems.at[i]).wait()

    def wait_one(ref, sem):
        pltpu.make_async_copy(ref, ref, sem).wait()

    def total(blocks, count):
        value = blocks[0]
        for i in range(1, count):
            value = value + blocks[i]
        return value

    def product(a, b):
        return (a[...].astype(F32) * b[...].astype(F32)).astype(BF16)

    for i in range(4):
        loads[i].wait()
    mixed, gmix = product(ig, va), product(go, og)
    for q in range(2):
        lanes = slice(q * ctx, (q + 1) * ctx)
        rows = dot_rows(by_channel[...], jnp.concatenate([mixed[:, lanes], gmix[:, lanes]], 1))
        there_out[pl.ds(q * part, part)] = rows.astype(BF16).reshape(part, 4, block)
    there_in[c] = there_out[c]
    near_sum[...] = jnp.sum(mixed.astype(F32) * gmix.astype(F32), axis=0, keepdims=True)
    near_recv[h] = near_sum[...]
    word[...] = jnp.zeros(word.shape, F32)

    pl.semaphore_wait(barrier, ctx - 1 + ahead)

    def send_piece(src, dst, sem):
        def send(t):
            pltpu.make_async_remote_copy(
                src_ref=src.at[t],
                dst_ref=dst.at[c],
                send_sem=send_sem.at[sem],
                recv_sem=recv_sem.at[sem],
                device_id=(d, t),
                device_id_type=MESH,
            ).start()

        return send

    send_there = send_piece(there_out, there_in, 0)
    send_all(near_peer, near, lambda t: near_sum, near_recv, h, 2)
    around(send_there, spots)
    within(send_there)
    wait_blocks(near_recv, near, recv_sem, 2)
    far_sum[...] = total(near_recv, near)
    far_recv[g] = far_sum[...]
    send_all(far_peer, far, lambda t: far_sum, far_recv, g, 3)
    for t in others:

        @pl.when(order(t) < ahead)
        def _():
            pltpu.make_async_remote_copy(
                src_ref=word,
                dst_ref=words.at[d],
                send_sem=wsend_sem.at[t],
                recv_sem=wrecv_sem.at[d],
                device_id=(t, c),
                device_id_type=MESH,
            ).start()

    def forward(table, x):
        section = dot(table, x)
        out = []
        for i in range(x.shape[1] // block):
            re = section[:outer, i * block : (i + 1) * block]
            im = section[outer:, i * block : (i + 1) * block]
            turned = jnp.concatenate(
                [
                    (re * cos[...] + im * sin[...]).astype(BF16),
                    (im * cos[...] - re * sin[...]).astype(BF16),
                ],
                1,
            )
            out.append(dot(turned, fwd[...]))
        return out

    def inverse(table, spectra):
        real, imag = [], []
        for spectrum in spectra:
            back = dot(spectrum, inv[...])
            re, im = back[:, :block], back[:, block:]
            real.append((re * cos[...] - im * sin[...]).astype(BF16))
            imag.append((im * cos[...] + re * sin[...]).astype(BF16))
        turned = jnp.concatenate([jnp.concatenate(real, 1), jnp.concatenate(imag, 1)], 0)
        return dot(table, turned).astype(BF16)

    for i in range(4, 12):
        loads[i].wait()
    entry[...] = entry_in[...].astype(BF16)
    fwd[...] = fwd_in[...].astype(BF16)
    for j in range(2):
        for a in range(ctx):
            taps_rows[j, pl.ds(a, 1)] = taps[pl.ds(j, 1), pl.ds(a * block, block)].astype(F32)
    both = jnp.concatenate([taps_rows[0], taps_rows[1]], 1).astype(BF16)
    for j, spectrum in enumerate(forward(entry[...], both)):
        kern[j] = spectrum
    inv[...] = inv_in[...].astype(BF16)
    leave[...] = leave_in[...].astype(BF16)

    wait_blocks(there_in, ctx, recv_sem, 0)
    halves = []
    for q in range(2):
        rows = there_in[pl.ds(q * part, part)].reshape(4 * part, block)
        halves.append(dot(of_piece[...], rows).astype(BF16))
    lines = [
        jnp.concatenate([rows[i * part : (i + 1) * part] for rows in halves], 0) for i in range(4)
    ]
    spectra = []
    for i in range(2):
        both = jnp.concatenate(lines[2 * i : 2 * i + 2], 1)
        spectra.append([(s[:, :block], s[:, block:]) for s in forward(entry[...], both)])
    sources, gradients = spectra

    specs = []
    for (ur, ui), (vr, vi) in zip(sources, gradients):
        specs.append(jnp.concatenate([ur * vr + ui * vi, ur * vi - ui * vr], 1).astype(BF16))
    term = inverse(leave[...], specs)
    for j in range(2):
        line = term[:, j * block : (j + 1) * block]
        fsend[:, j] = line.reshape(n_dp, ctx // n_dp, block)

    def send_share(src, dst, out, come, t):
        pltpu.make_async_remote_copy(
            src_ref=src,
            dst_ref=dst.at[d],
            send_sem=out.at[t],
            recv_sem=come.at[d],
            device_id=(t, c),
            device_id_type=MESH,
        ).start()

    def send_filter(t):
        send_share(fsend.at[t], frecv, fsend_sem, frecv_sem, t)

    def send_sum(t):
        send_share(dp_sum, dp_recv, dsend_sem, drecv_sem, t)

    pl.when(ahead > 0)(functools.partial(send_filter, 0))
    frecv[d] = fsend[d]
    wait_blocks(far_recv, far, recv_sem, 3)
    dp_sum[...] = total(far_recv, far)
    pl.when(ahead > 0)(functools.partial(send_sum, 0))
    dp_recv[d] = dp_sum[...]

    kernels = [(kern[j][:, :block], kern[j][:, block:]) for j in range(2)]
    convs, backs = [], []
    for (ur, ui), (vr, vi), (kr, ki) in zip(sources, gradients, kernels):
        convs.append(jnp.concatenate([ur * kr - ui * ki, ur * ki + ui * kr], 1).astype(BF16))
        backs.append(jnp.concatenate([kr * vr + ki * vi, kr * vi - ki * vr], 1).astype(BF16))
    lines = []
    for specs in (convs, backs):
        both = inverse(leave[...], specs)
        lines += [both[:, :block], both[:, block:]]
    for q in range(2):
        rows = jnp.concatenate([x[q * part : (q + 1) * part] for x in lines], 0)
        rows = dot(by_piece[...], rows).astype(BF16)
        back_out[pl.ds(q * part, part)] = rows.reshape(part, 4, block)
    back_in[c] = back_out[c]

    @pl.when(ahead > 1)
    def _():
        send_filter(1)
        send_sum(1)

    send_back = send_piece(back_out, back_in, 1)
    around(send_back, spots)
    within(send_back)

    for t in others[::-1]:

        @pl.when(order(t) > ahead)
        def _():
            wait_one(words.at[t], wrecv_sem.at[t])

        @pl.when((t > 1) | ((t == 1) & (ahead <= 1)))
        def _():
            send_filter(t)
            send_sum(t)

    wait_blocks(back_in, ctx, recv_sem, 1)
    eye = selector(block, lambda r: r)
    convs, backs = [], []
    for q in range(2):
        rows = back_in[pl.ds(q * part, part)].reshape(4 * part, block)
        rows = dot(dot_rows(eye, rows).astype(BF16), by_channel[...])
        convs.append(rows[:, :ctx])
        backs.append(rows[:, ctx:])
    gains = gain[...]
    gout[...] = (
        go[...].astype(F32)
        * (jnp.concatenate(convs, 1) + gains * product(ig, va).astype(F32))
    ).astype(BF16)
    grad_mixed = jnp.concatenate(backs, 1) + gains * product(go, og).astype(F32)
    gin[...] = (grad_mixed * va[...].astype(F32)).astype(BF16)
    gval[...] = (grad_mixed * ig[...].astype(F32)).astype(BF16)

    for t in others:
        wait_one(frecv.at[t], frecv_sem.at[t])
    scale = 1.0 / math.sqrt(n_dp * ctx * block)
    grad = frecv[0].astype(F32)
    for i in range(1, n_dp):
        grad = grad + frecv[i].astype(F32)
    grad = grad * scale
    for j in range(2):
        for a in range(ctx // n_dp):
            filter_out[pl.ds(j, 1), pl.ds(a * block, block)] = grad[j, a : a + 1]
    for t in others:
        wait_one(dp_recv.at[t], drecv_sem.at[t])
    skip_out[...] = total(dp_recv, n_dp) * scale

    wait_blocks(there_in, ctx, send_sem, 0)
    wait_blocks(back_in, ctx, send_sem, 1)
    wait_blocks(near_recv, near, send_sem, 2)
    wait_blocks(far_recv, far, send_sem, 3)
    for t in others:
        wait_one(fsend.at[t], fsend_sem.at[t])
        wait_one(dp_sum, dsend_sem.at[t])

        @pl.when(order(t) < ahead)
        def _():
            wait_one(word, wsend_sem.at[t])


def copy_kernel(*refs):
    n = (len(refs) - 1) // 2
    copies = [pltpu.make_async_copy(refs[i], refs[n + i], refs[-1].at[i]) for i in range(n)]
    for copy in copies:
        copy.start()
    for copy in copies:
        copy.wait()


def per_device(input_gate, values, output_gate, grad_out, filter_taps, skip_gain):
    n_dp = lax.axis_size("dp")
    ctx = lax.axis_size("context")
    far, near = group_sizes(ctx)
    block, chans = input_gate.shape[1:]
    tables = dft_tables(ctx, block, 1.0 / (2 * ctx * block))
    gates = (input_gate[0], values[0], output_gate[0], grad_out[0], skip_gain.reshape(1, -1))
    operands = gates + (filter_taps,) + tables
    share = ctx // n_dp
    outs = tuple(jax.ShapeDtypeStruct((block, chans), BF16) for _ in range(3)) + (
        jax.ShapeDtypeStruct((2, share * block), F32),
        jax.ShapeDtypeStruct((1, chans), F32),
    )
    vmem = pltpu.VMEM
    dma = pltpu.SemaphoreType.DMA
    results = pl.pallas_call(
        functools.partial(mixer_kernel, (n_dp, far, near, chans, block)),
        out_shape=tuple(pltpu.VMEM(x.shape, x.dtype) for x in outs),
        in_specs=[pl.BlockSpec(memory_space=pltpu.HBM)] * len(operands),
        out_specs=tuple(pl.BlockSpec(memory_space=pltpu.VMEM) for _ in outs),
        scratch_shapes=[vmem(x.shape, x.dtype) for x in operands]
        + [vmem((2, ctx, block), F32)]
        + [vmem(tables[i].shape, BF16) for i in (0, 3, 4, 5)]
        + [vmem((2 * ctx, 2 * ctx), BF16)] * 3
        + [vmem((ctx, 4, block), BF16)] * 4
        + [vmem((1, chans), F32), vmem((near, 1, chans), F32)]
        + [vmem((1, chans), F32), vmem((far, 1, chans), F32)]
        + [vmem((n_dp, 2, share, block), BF16)] * 2
        + [vmem((1, chans), F32), vmem((n_dp, 1, chans), F32)]
        + [vmem((1, 128), F32), vmem((n_dp, 1, 128), F32)]
        + [vmem((2, 2 * ctx, 2 * block), F32)]
        + [dma((len(operands),)), dma((4,)), dma((4,))]
        + [dma((n_dp,))] * 6,
        compiler_params=pltpu.CompilerParams(
            collective_id=0, has_side_effects=True, vmem_limit_bytes=32 * 1024 * 1024
        ),
        name="mixer",
    )(*(pltpu.with_memory_space_constraint(x, pltpu.HBM) for x in operands))
    grad_input, grad_value, grad_output, filter_grad, skip_grad = pl.pallas_call(
        copy_kernel,
        out_shape=outs,
        in_specs=[pl.BlockSpec(memory_space=pltpu.VMEM)] * len(outs),
        out_specs=tuple(pl.BlockSpec(memory_space=pl.ANY) for _ in outs),
        scratch_shapes=[dma((len(outs),))],
        compiler_params=pltpu.CompilerParams(vmem_limit_bytes=32 * 1024 * 1024),
        name="results",
    )(*results)
    return (
        grad_input[None],
        grad_value[None],
        grad_output[None],
        filter_grad,
        skip_grad.reshape(-1),
    )


def solution(mesh):
    return jax.shard_map(
        per_device,
        mesh=mesh,
        in_specs=(
            P("dp", "context", None),
            P("dp", "context", None),
            P("dp", "context", None),
            P("dp", "context", None),
            P("context", None),
            P(),
        ),
        out_specs=(
            P("dp", "context", None),
            P("dp", "context", None),
            P("dp", "context", None),
            P("context", "dp"),
            P(),
        ),
        check_vma=False,
    )
```

```python
import functools
import math

import jax
import jax.numpy as jnp
import numpy as np
from jax import lax
from jax.experimental import pallas as pl
from jax.experimental.pallas import tpu as pltpu
from jax.sharding import PartitionSpec as P

MESH = pl.DeviceIdType.MESH
F32 = jnp.float32
BF16 = jnp.bfloat16


def group_sizes(context):
    near = 1
    while 2 * near * near * 2 <= context:
        near *= 2
    return context // near, near


def dft_tables(pieces, block_len, scale):
    outer = 2 * pieces
    total = outer * block_len

    def angle(first, second, modulus):
        return (first[:, None] * second[None, :] % modulus) * (2.0 * math.pi / modulus)

    across = np.arange(pieces)
    outer_index = np.arange(outer)
    inner_index = np.arange(block_len)
    first = angle(outer_index, across, outer)
    entry = np.concatenate([np.cos(first), -np.sin(first)], 0)
    twist = angle(outer_index, inner_index, total)
    twist_cos, twist_sin = np.cos(twist), np.sin(twist)
    inner = angle(inner_index, inner_index, block_len)
    cosine, sine = np.cos(inner), np.sin(inner)
    forward_inner = np.block([[cosine, -sine], [sine, cosine]])
    inverse_inner = np.block([[cosine, sine], [-sine, cosine]])
    last = angle(across, outer_index, outer)
    leave = np.concatenate([np.cos(last), -np.sin(last)], 1) * scale

    def low(table):
        return table.astype(BF16).astype(np.float32)

    return (
        low(entry),
        twist_cos.astype(np.float32),
        twist_sin.astype(np.float32),
        low(forward_inner),
        low(inverse_inner),
        low(leave),
    )


def dot(a, b):
    return jnp.dot(a, b, preferred_element_type=F32)


def dot_rows(a, b):
    return lax.dot_general(a, b, (((1,), (1,)), ((), ())), preferred_element_type=F32)


def selector(n, place):
    row = lax.broadcasted_iota(jnp.int32, (n, n), 0)
    col = lax.broadcasted_iota(jnp.int32, (n, n), 1)
    return (col == place(row)).astype(BF16)


def mixer_kernel(
    sizes,
    ig_hbm, va_hbm, og_hbm, go_hbm, gain_hbm, taps_hbm, entry_hbm, cos_hbm, sin_hbm, fwd_hbm,
    inv_hbm, leave_hbm,
    gin, gval, gout, filter_out, skip_out,
    ig, va, og, go, gain, taps, entry_in, cos, sin, fwd_in, inv_in, leave_in,
    taps_rows, entry, fwd, inv, leave, by_channel, by_piece, of_piece,
    there_out, there_in, back_out, back_in,
    near_sum, near_recv, far_sum, far_recv, fsend, frecv, dp_sum, dp_recv, word, words, kern,
    load_sem, send_sem, recv_sem, fsend_sem, frecv_sem, dsend_sem, drecv_sem,
    wsend_sem, wrecv_sem,
):
    n_dp, far, near, chans, block = sizes
    ctx = far * near
    outer = 2 * ctx
    d = lax.axis_index("dp")
    c = lax.axis_index("context")
    g = c // near
    h = c % near

    pairs = (
        (ig_hbm, ig), (va_hbm, va), (og_hbm, og), (go_hbm, go), (taps_hbm, taps),
        (entry_hbm, entry_in), (cos_hbm, cos), (sin_hbm, sin), (fwd_hbm, fwd_in),
        (inv_hbm, inv_in), (leave_hbm, leave_in), (gain_hbm, gain),
    )
    loads = [pltpu.make_async_copy(src, dst, load_sem.at[i]) for i, (src, dst) in enumerate(pairs)]

    def far_peer(i):
        t = lax.rem(g + i, far)
        return t, (d, t * near + h)

    def near_peer(i):
        t = lax.rem(h + i, near)
        return t, (d, g * near + t)

    n_y = int(math.isqrt(far))
    n_z, n_x = far // n_y, near // 2
    z, y, x, core = g // n_y, lax.rem(g, n_y), h // 2, lax.rem(h, 2)
    turns_y = sorted(range(n_y), key=lambda v: -min(v, n_y - v))
    turns_x = sorted(range(n_x), key=lambda v: -min(v, n_x - v))
    spots = [(i, j) for i in turns_x for j in (1, 0)]

    def around(act, spots):
        def step(s, carry):
            there = s + (1 - z // (n_z // 2)) * (n_z - 1 - 2 * s)
            for turn in turns_y:
                row = there * n_y + lax.rem(y + turn, n_y)

                def go():
                    for i, j in spots:
                        act(row * near + lax.rem(x + i, n_x) * 2 + lax.rem(core + j, 2))

                if turn == 0:
                    pl.when(row != g)(go)
                else:
                    go()
            return carry

        lax.fori_loop(0, n_z, step, 0)

    def within(act):
        for i, j in spots[:-1]:
            act(g * near + lax.rem(x + i, n_x) * 2 + lax.rem(core + j, 2))

    barrier = pltpu.get_barrier_semaphore()

    def greet(t):
        pl.semaphore_signal(barrier, inc=1, device_id=(d, t), device_id_type=MESH)

    half = n_dp // 2

    def order(t):
        return t + (t // half) * (half - 1 - 2 * lax.rem(t, half))

    ahead = order(d)
    others = [lax.rem(d + n_dp - i, n_dp) for i in (2, 1, 3)[: n_dp - 1]] if n_dp > 2 else [1 - d]
    for load in loads[:4]:
        load.start()
    around(greet, spots)
    within(greet)
    for t in others:

        @pl.when(order(t) > ahead)
        def _():
            pl.semaphore_signal(barrier, inc=1, device_id=(t, c), device_id_type=MESH)

    for load in loads[4:]:
        load.start()

    part = ctx // 2
    by_channel[...] = selector(
        4 * part, lambda r: (r % 4) // 2 * ctx + r // 4 * 2 + r % 2
    )
    by_piece[...] = selector(4 * part, lambda r: r % 4 * part + r // 4)
    of_piece[...] = selector(4 * part, lambda r: r % part * 4 + r // part)

    def send_all(peer, count, src, dst, own, sem):
        def step(i, carry):
            t, target = peer(i)
            pltpu.make_async_remote_copy(
                src_ref=src(t),
                dst_ref=dst.at[own],
                send_sem=send_sem.at[sem],
                recv_sem=recv_sem.at[sem],
                device_id=target,
                device_id_type=MESH,
            ).start()
            return carry

        lax.fori_loop(1, count, step, 0)

    def wait_blocks(dst, count, sems, i):
        blocks = dst.at[pl.ds(0, count - 1)]
        pltpu.make_async_copy(blocks, blocks, sems.at[i]).wait()

    def wait_one(ref, sem):
        pltpu.make_async_copy(ref, ref, sem).wait()

    def total(blocks, count):
        value = blocks[0]
        for i in range(1, count):
            value = value + blocks[i]
        return value

    def product(a, b):
        return (a[...].astype(F32) * b[...].astype(F32)).astype(BF16)

    for i in range(4):
        loads[i].wait()
    mixed, gmix = product(ig, va), product(go, og)
    for q in range(2):
        lanes = slice(q * ctx, (q + 1) * ctx)
        rows = dot_rows(by_channel[...], jnp.concatenate([mixed[:, lanes], gmix[:, lanes]], 1))
        there_out[pl.ds(q * part, part)] = rows.astype(BF16).reshape(part, 4, block)
    there_in[c] = there_out[c]
    near_sum[...] = jnp.sum(mixed.astype(F32) * gmix.astype(F32), axis=0, keepdims=True)
    near_recv[h] = near_sum[...]
    word[...] = jnp.zeros(word.shape, F32)

    pl.semaphore_wait(barrier, ctx - 1 + ahead)

    def send_piece(src, dst, sem):
        def send(t):
            pltpu.make_async_remote_copy(
                src_ref=src.at[t],
                dst_ref=dst.at[c],
                send_sem=send_sem.at[sem],
                recv_sem=recv_sem.at[sem],
                device_id=(d, t),
                device_id_type=MESH,
            ).start()

        return send

    send_there = send_piece(there_out, there_in, 0)
    send_all(near_peer, near, lambda t: near_sum, near_recv, h, 2)
    around(send_there, spots)
    within(send_there)
    for t in others:

        @pl.when(order(t) < ahead)
        def _():
            pltpu.make_async_remote_copy(
                src_ref=word,
                dst_ref=words.at[d],
                send_sem=wsend_sem.at[t],
                recv_sem=wrecv_sem.at[d],
                device_id=(t, c),
                device_id_type=MESH,
            ).start()

    wait_blocks(near_recv, near, recv_sem, 2)
    far_sum[...] = total(near_recv, near)
    far_recv[g] = far_sum[...]
    send_all(far_peer, far, lambda t: far_sum, far_recv, g, 3)

    def forward(table, x):
        section = dot(table, x)
        out = []
        for i in range(x.shape[1] // block):
            re = section[:outer, i * block : (i + 1) * block]
            im = section[outer:, i * block : (i + 1) * block]
            turned = jnp.concatenate(
                [
                    (re * cos[...] + im * sin[...]).astype(BF16),
                    (im * cos[...] - re * sin[...]).astype(BF16),
                ],
                1,
            )
            out.append(dot(turned, fwd[...]))
        return out

    def inverse(table, spectra):
        real, imag = [], []
        for spectrum in spectra:
            back = dot(spectrum, inv[...])
            re, im = back[:, :block], back[:, block:]
            real.append((re * cos[...] - im * sin[...]).astype(BF16))
            imag.append((im * cos[...] + re * sin[...]).astype(BF16))
        turned = jnp.concatenate([jnp.concatenate(real, 1), jnp.concatenate(imag, 1)], 0)
        return dot(table, turned).astype(BF16)

    for i in range(4, 12):
        loads[i].wait()
    entry[...] = entry_in[...].astype(BF16)
    fwd[...] = fwd_in[...].astype(BF16)
    for j in range(2):
        for a in range(ctx):
            taps_rows[j, pl.ds(a, 1)] = taps[pl.ds(j, 1), pl.ds(a * block, block)].astype(F32)
    both = jnp.concatenate([taps_rows[0], taps_rows[1]], 1).astype(BF16)
    for j, spectrum in enumerate(forward(entry[...], both)):
        kern[j] = spectrum
    inv[...] = inv_in[...].astype(BF16)
    leave[...] = leave_in[...].astype(BF16)

    wait_blocks(there_in, ctx, recv_sem, 0)
    halves = []
    for q in range(2):
        rows = there_in[pl.ds(q * part, part)].reshape(4 * part, block)
        halves.append(dot(of_piece[...], rows).astype(BF16))
    lines = [
        jnp.concatenate([rows[i * part : (i + 1) * part] for rows in halves], 0) for i in range(4)
    ]
    spectra = []
    for i in range(2):
        both = jnp.concatenate(lines[2 * i : 2 * i + 2], 1)
        spectra.append([(s[:, :block], s[:, block:]) for s in forward(entry[...], both)])
    sources, gradients = spectra

    specs = []
    for (ur, ui), (vr, vi) in zip(sources, gradients):
        specs.append(jnp.concatenate([ur * vr + ui * vi, ur * vi - ui * vr], 1).astype(BF16))
    term = inverse(leave[...], specs)
    for j in range(2):
        line = term[:, j * block : (j + 1) * block]
        fsend[:, j] = line.reshape(n_dp, ctx // n_dp, block)

    def send_share(src, dst, out, come, t):
        pltpu.make_async_remote_copy(
            src_ref=src,
            dst_ref=dst.at[d],
            send_sem=out.at[t],
            recv_sem=come.at[d],
            device_id=(t, c),
            device_id_type=MESH,
        ).start()

    def send_filter(t):
        send_share(fsend.at[t], frecv, fsend_sem, frecv_sem, t)

    def send_sum(t):
        send_share(dp_sum, dp_recv, dsend_sem, drecv_sem, t)

    pl.when(ahead > 0)(functools.partial(send_filter, 0))
    frecv[d] = fsend[d]
    wait_blocks(far_recv, far, recv_sem, 3)
    dp_sum[...] = total(far_recv, far)
    pl.when(ahead > 0)(functools.partial(send_sum, 0))
    dp_recv[d] = dp_sum[...]

    kernels = [(kern[j][:, :block], kern[j][:, block:]) for j in range(2)]
    convs, backs = [], []
    for (ur, ui), (vr, vi), (kr, ki) in zip(sources, gradients, kernels):
        convs.append(jnp.concatenate([ur * kr - ui * ki, ur * ki + ui * kr], 1).astype(BF16))
        backs.append(jnp.concatenate([kr * vr + ki * vi, kr * vi - ki * vr], 1).astype(BF16))
    lines = []
    for specs in (convs, backs):
        both = inverse(leave[...], specs)
        lines += [both[:, :block], both[:, block:]]
    for q in range(2):
        rows = jnp.concatenate([x[q * part : (q + 1) * part] for x in lines], 0)
        rows = dot(by_piece[...], rows).astype(BF16)
        back_out[pl.ds(q * part, part)] = rows.reshape(part, 4, block)
    back_in[c] = back_out[c]

    @pl.when(ahead > 1)
    def _():
        send_filter(1)
        send_sum(1)

    send_back = send_piece(back_out, back_in, 1)
    around(send_back, spots)
    within(send_back)

    for t in others[::-1]:

        @pl.when(order(t) > ahead)
        def _():
            wait_one(words.at[t], wrecv_sem.at[t])

        @pl.when((t > 1) | ((t == 1) & (ahead <= 1)))
        def _():
            send_filter(t)
            send_sum(t)

    wait_blocks(back_in, ctx, recv_sem, 1)
    eye = selector(block, lambda r: r)
    convs, backs = [], []
    for q in range(2):
        rows = back_in[pl.ds(q * part, part)].reshape(4 * part, block)
        rows = dot(dot_rows(eye, rows).astype(BF16), by_channel[...])
        convs.append(rows[:, :ctx])
        backs.append(rows[:, ctx:])
    gains = gain[...]
    gout[...] = (
        go[...].astype(F32)
        * (jnp.concatenate(convs, 1) + gains * product(ig, va).astype(F32))
    ).astype(BF16)
    grad_mixed = jnp.concatenate(backs, 1) + gains * product(go, og).astype(F32)
    gin[...] = (grad_mixed * va[...].astype(F32)).astype(BF16)
    gval[...] = (grad_mixed * ig[...].astype(F32)).astype(BF16)

    for t in others:
        wait_one(frecv.at[t], frecv_sem.at[t])
    scale = 1.0 / math.sqrt(n_dp * ctx * block)
    grad = frecv[0].astype(F32)
    for i in range(1, n_dp):
        grad = grad + frecv[i].astype(F32)
    grad = grad * scale
    for j in range(2):
        for a in range(ctx // n_dp):
            filter_out[pl.ds(j, 1), pl.ds(a * block, block)] = grad[j, a : a + 1]
    for t in others:
        wait_one(dp_recv.at[t], drecv_sem.at[t])
    skip_out[...] = total(dp_recv, n_dp) * scale

    wait_blocks(there_in, ctx, send_sem, 0)
    wait_blocks(back_in, ctx, send_sem, 1)
    wait_blocks(near_recv, near, send_sem, 2)
    wait_blocks(far_recv, far, send_sem, 3)
    for t in others:
        wait_one(fsend.at[t], fsend_sem.at[t])
        wait_one(dp_sum, dsend_sem.at[t])

        @pl.when(order(t) < ahead)
        def _():
            wait_one(word, wsend_sem.at[t])


def copy_kernel(*refs):
    n = (len(refs) - 1) // 2
    copies = [pltpu.make_async_copy(refs[i], refs[n + i], refs[-1].at[i]) for i in range(n)]
    for copy in copies:
        copy.start()
    for copy in copies:
        copy.wait()


def per_device(input_gate, values, output_gate, grad_out, filter_taps, skip_gain):
    n_dp = lax.axis_size("dp")
    ctx = lax.axis_size("context")
    far, near = group_sizes(ctx)
    block, chans = input_gate.shape[1:]
    tables = dft_tables(ctx, block, 1.0 / (2 * ctx * block))
    gates = (input_gate[0], values[0], output_gate[0], grad_out[0], skip_gain.reshape(1, -1))
    operands = gates + (filter_taps,) + tables
    share = ctx // n_dp
    outs = tuple(jax.ShapeDtypeStruct((block, chans), BF16) for _ in range(3)) + (
        jax.ShapeDtypeStruct((2, share * block), F32),
        jax.ShapeDtypeStruct((1, chans), F32),
    )
    vmem = pltpu.VMEM
    dma = pltpu.SemaphoreType.DMA
    results = pl.pallas_call(
        functools.partial(mixer_kernel, (n_dp, far, near, chans, block)),
        out_shape=tuple(pltpu.VMEM(x.shape, x.dtype) for x in outs),
        in_specs=[pl.BlockSpec(memory_space=pltpu.HBM)] * len(operands),
        out_specs=tuple(pl.BlockSpec(memory_space=pltpu.VMEM) for _ in outs),
        scratch_shapes=[vmem(x.shape, x.dtype) for x in operands]
        + [vmem((2, ctx, block), F32)]
        + [vmem(tables[i].shape, BF16) for i in (0, 3, 4, 5)]
        + [vmem((2 * ctx, 2 * ctx), BF16)] * 3
        + [vmem((ctx, 4, block), BF16)] * 4
        + [vmem((1, chans), F32), vmem((near, 1, chans), F32)]
        + [vmem((1, chans), F32), vmem((far, 1, chans), F32)]
        + [vmem((n_dp, 2, share, block), BF16)] * 2
        + [vmem((1, chans), F32), vmem((n_dp, 1, chans), F32)]
        + [vmem((1, 128), F32), vmem((n_dp, 1, 128), F32)]
        + [vmem((2, 2 * ctx, 2 * block), F32)]
        + [dma((len(operands),)), dma((4,)), dma((4,))]
        + [dma((n_dp,))] * 6,
        compiler_params=pltpu.CompilerParams(
            collective_id=0, has_side_effects=True, vmem_limit_bytes=32 * 1024 * 1024
        ),
        name="mixer",
    )(*(pltpu.with_memory_space_constraint(x, pltpu.HBM) for x in operands))
    grad_input, grad_value, grad_output, filter_grad, skip_grad = pl.pallas_call(
        copy_kernel,
        out_shape=outs,
        in_specs=[pl.BlockSpec(memory_space=pltpu.VMEM)] * len(outs),
        out_specs=tuple(pl.BlockSpec(memory_space=pl.ANY) for _ in outs),
        scratch_shapes=[dma((len(outs),))],
        compiler_params=pltpu.CompilerParams(vmem_limit_bytes=32 * 1024 * 1024),
        name="results",
    )(*results)
    return (
        grad_input[None],
        grad_value[None],
        grad_output[None],
        filter_grad,
        skip_grad.reshape(-1),
    )


def solution(mesh):
    return jax.shard_map(
        per_device,
        mesh=mesh,
        in_specs=(
            P("dp", "context", None),
            P("dp", "context", None),
            P("dp", "context", None),
            P("dp", "context", None),
            P("context", None),
            P(),
        ),
        out_specs=(
            P("dp", "context", None),
            P("dp", "context", None),
            P("dp", "context", None),
            P("context", "dp"),
            P(),
        ),
        check_vma=False,
    )
```
